128 devices in a mesh: res: 32 (over x, y, core), head: 4 (over z).
Axes of the slice: x: 4, y: 4, z: 4, core: 2. Of those that a mesh axis runs over, the one named last changes fastest.
Arguments:
- queries: bfloat16 [8192, 3072], P(('res', 'head'))
- keys: bfloat16 [8192, 3072], P(('res', 'head'))
- values: bfloat16 [8192, 3072], P(('res', 'head')), may hold values from -6 to 6
- out_grad: bfloat16 [8192, 3072], P('res', 'head'), may hold values from -6 to 6
- chain_bias: float32 [24], P('head'), may hold values from -2 to 1
- chain_of_block: int32 [64], P('res'), may hold values from 0 to 15, never falling along the last dimension, each value on 1 to 8 neighbouring positions
- key_valid: int32 [8192], P('res'), may hold values from 0 to 1, as said below
- neighbours: int32 [64, 16], P('res'), may hold values from 0 to 63, as said below
Outputs:
- attended: bfloat16 [8192, 3072], P('res', 'head')
- query_grad: bfloat16 [8192, 3072], P(('res', 'head'))
- key_grad: bfloat16 [8192, 3072], P(('res', 'head'))
- value_grad: bfloat16 [8192, 3072], P(('res', 'head'))
The draws below stay inside these ranges and needn't reach their ends.
Inputs may be any that keep to these rules, and one draw needn't show every extreme that they name: `neighbours`: each row b lists 16 distinct blocks, b itself among them. Over the 2 blocks of one group, the distinct blocks listed from any one other group number at most 1, and exactly 1 for some pair of groups in every draw. `key_valid`: residues 0 and 1 of every block hold 1.
All inputs are finite; a program needn't handle non-finite values.
Results may differ from the reference program's by a relative error of at most 0.012.
The reference program's roundings to bfloat16 on the way (of `rounded`, `dscore` and `probs_round`) count: a program that leaves them out, or rounds other values in their place, can miss the bound.
Values may be sent and summed in bfloat16 or wider, within the bound.
No kernel may reach another device: no remote copies, remote signals or barrier semaphores. Data moves between devices by JAX's collectives and lax.ppermute only.
A program may use at most 192 MiB of HBM per device.

```python
import math
import jax
import jax.numpy as jnp
import numpy as np
from jax import lax

BS = 128
H = 24
HD = 128
NBR = 16
BLK = 2
NB = 64
N = 8192
CAP = 1
CHAINS = 16
N_RES = 32


def key_field(key):
    field = jnp.clip(jax.random.normal(key, (NB, BS, H * HD), jnp.float32), -6.0, 6.0)
    position = jnp.arange(BS)[None, :, None]
    first_row = field[:, 0:1, :]
    field = jnp.where(position == 0, first_row, field)
    field = jnp.where(position == 1, field, field)
    return field


def neighbour_lists(key):
    key = jax.random.fold_in(key, 11)
    first_key, second_key = jax.random.split(key)
    groups = NB // BLK
    others = groups - 1
    within = jax.random.randint(first_key, (groups, others, BLK), 0, 1 << 20) * BLK + jnp.arange(BLK)
    chosen = jnp.argsort(within, axis=-1, stable=True)[..., :CAP]
    owners = (jnp.arange(groups)[:, None] + 1 + jnp.arange(others)[None, :]) % groups
    candidates = (owners[:, :, None] * BLK + chosen).reshape(groups, others * CAP)
    count = others * CAP
    remote_count = NBR - BLK
    scores = jax.random.randint(second_key, (groups, BLK, count), 0, 1 << 20) * count + jnp.arange(count)
    picks = jnp.argsort(scores, axis=-1, stable=True)[..., :remote_count]
    leading = jnp.broadcast_to(jnp.arange(remote_count)[None, None, :], picks.shape)
    picks = jnp.where(jnp.arange(BLK)[None, :, None] == 0, leading, picks)
    remote = jnp.take_along_axis(jnp.broadcast_to(candidates[:, None, :], (groups, BLK, count)), picks, axis=-1)
    local = jnp.arange(groups)[:, None, None] * BLK + (jnp.arange(BLK)[None, :, None] + jnp.arange(BLK)[None, None, :]) % BLK
    return jnp.concatenate([local, remote], axis=-1).reshape(NB, NBR).astype(jnp.int32)


def draw_keys(key, part):
    field = key_field(key)
    return field.reshape(N, H * HD).astype(jnp.bfloat16)


def draw_queries(key, part):
    key = jax.random.fold_in(key, 14)
    result = jnp.clip(jax.random.normal(key, (NB, BS, H * HD), jnp.float32), -6.0, 6.0)
    return result.reshape(N, H * HD).astype(jnp.bfloat16)


def draw_key_valid(key, part):
    key = jax.random.fold_in(key, 12)
    first_key, second_key, third_key = jax.random.split(key, 3)
    drawn = jax.random.randint(first_key, (NB, BS), 0, 20) >= 3
    padded_block = jax.random.randint(second_key, (NB,), 0, 4) == 0
    tail = jax.random.randint(third_key, (NB,), 0, BS // 2)
    position = jnp.arange(BS)[None, :]
    padding = padded_block[:, None] & (position >= BS - tail[:, None])
    valid = drawn & jnp.logical_not(padding) | (position < 2)
    return valid.reshape(N).astype(jnp.int32)


def draw_neighbours(key, part):
    lists = neighbour_lists(key)
    return lists


def level_of(stream_key, shape, shards, smallest, top_value):
    gain = 1.0
    for dim, parts in shards:
        draws = jax.random.uniform(jax.random.fold_in(jax.random.fold_in(stream_key, 6), dim), (parts,), jnp.float32, smallest / len(shards), top_value / len(shards))
        gain = gain * jnp.repeat(jnp.exp(draws), shape[dim] // parts).reshape((-1,) + (1,) * (len(shape) - 1 - dim))
    return gain


def split_up(number_of, total, limit, lean):
    weights = [(1 << 20) // math.isqrt(standing ** lean) + 1 for standing in range(2, number_of + 1)]
    rest, given = total - limit - (number_of - 1), [1] * (number_of - 1)
    while rest > 0:
        free = [i for i in range(number_of - 1) if given[i] < limit]
        mass, budget = sum([weights[i] for i in free]), rest
        for i in free:
            addition = min(limit - given[i], max(1, budget * weights[i] // mass), rest)
            given[i] = given[i] + addition
            rest = rest - addition
    return np.array([limit] + given)


def uneven_parts(stream_key, count, total, most, slope):
    if count == 2:
        one = jax.random.randint(stream_key, (), max(1, total - most), min(most, total - 1) + 1)
        return jnp.stack([one, total - one])
    sizes = jnp.asarray(split_up(count, total, most, slope), jnp.int32)
    pairs = (count - 1) // 2
    giver, receiver = sizes[1:1 + 2 * pairs:2], sizes[2:2 + 2 * pairs:2]
    margin = jnp.minimum(giver - 1, most - receiver)
    moved = jax.random.randint(jax.random.fold_in(stream_key, 1), (pairs,), 0, 1 << 20) % (margin + 1)
    sizes = sizes.at[1:1 + 2 * pairs:2].set(giver - moved).at[2:2 + 2 * pairs:2].set(receiver + moved)
    return sizes[jax.random.permutation(jax.random.fold_in(stream_key, 2), count)]


def normal_values(key, dims, scale, limit, cuts=(), held_as=jnp.bfloat16):
    values = jax.random.normal(key, dims, jnp.float32) * scale
    if len(cuts) > 0:
        values = level_of(key, dims, cuts, -0.22, 0.18) * values
    return jnp.clip(values, min=-limit, max=limit).astype(held_as)


def setup_inputs(seed: int = 0) -> dict:
    arg_keys = jax.random.split(jax.random.key(seed), 9)
    return {
        "queries": draw_queries(jax.random.fold_in(arg_keys[8], 71), 0),
        "keys": draw_keys(jax.random.fold_in(arg_keys[8], 71), 0),
        "values": normal_values(arg_keys[2], (N, H * HD), 1.0, 6.0, ((0, 128),)),
        "out_grad": normal_values(arg_keys[3], (N, H * HD), 1.0, 6.0, ((0, 32), (1, 4))),
        "chain_bias": jnp.clip(-2.0 + 3.0 * jax.random.uniform(arg_keys[4], (H,), jnp.float32) ** level_of(arg_keys[4], (H,), ((0, 4),), -0.2, 0.2), -2.0, 1.0),
        "chain_of_block": jnp.searchsorted(jnp.cumsum(uneven_parts(arg_keys[5], CHAINS, NB, 8, 0)), jnp.arange(NB), side="right").astype(jnp.int32),
        "key_valid": draw_key_valid(jax.random.fold_in(arg_keys[8], 71), 0),
        "neighbours": draw_neighbours(jax.random.fold_in(arg_keys[8], 71), 0),
    }


def bfloat_round(value):
    return lax.optimization_barrier(value.astype(jnp.bfloat16)).astype(jnp.float32)

def reference(queries, keys, values, out_grad, chain_bias, chain_of_block, key_valid, neighbours):
    scale = 1.0 / math.sqrt(HD)
    width = H * HD
    query_blocks = queries.reshape(NB, BS, H, HD)
    key_blocks = keys.reshape(NB, BS, H, HD)
    value_blocks = values.reshape(NB, BS, H, HD)
    grad_blocks = out_grad.reshape(NB, BS, H, HD)
    codes = jnp.where(key_valid.reshape(NB, BS) == 1, chain_of_block[:, None], -1).astype(jnp.int32)
    block_owner = jnp.arange(NB, dtype=jnp.int32) // BLK

    def one_group(carry, group):
        key_sum, value_sum = carry
        first = (group * BLK).astype(jnp.int32)
        lists = lax.dynamic_slice_in_dim(neighbours, first, BLK, 0)
        flat = lists.reshape(-1)
        query_here = lax.dynamic_slice_in_dim(query_blocks, first, BLK, 0).astype(jnp.float32)
        grad_here = lax.dynamic_slice_in_dim(grad_blocks, first, BLK, 0).astype(jnp.float32)
        chain_here = lax.dynamic_slice_in_dim(chain_of_block, first, BLK, 0)
        key_near = jnp.take(key_blocks, flat, axis=0).astype(jnp.float32).reshape(BLK, NBR * BS, H, HD)
        value_near = jnp.take(value_blocks, flat, axis=0).astype(jnp.float32).reshape(BLK, NBR * BS, H, HD)
        code_near = jnp.take(codes, flat, axis=0).reshape(BLK, NBR * BS)
        valid = code_near >= 0
        cross = (code_near != chain_here[:, None]).astype(jnp.float32)
        scores = jnp.einsum('jqhd,jkhd->jhqk', query_here, key_near) * scale
        scores = scores + chain_bias[None, :, None, None] * cross[:, None, None, :]
        scores = jnp.where(valid[:, None, None, :], scores, -jnp.inf)
        peak = lax.optimization_barrier(jnp.max(scores, axis=-1, keepdims=True))
        weights = jnp.exp(scores - peak)
        total = lax.optimization_barrier(jnp.sum(weights, axis=-1, keepdims=True))
        rounded = bfloat_round(weights)
        mixed = jnp.einsum('jhqk,jkhd->jhqd', rounded, value_near) / total
        attended_here = jnp.transpose(mixed, (0, 2, 1, 3)).astype(jnp.bfloat16)
        delta = lax.optimization_barrier(jnp.sum(grad_here * attended_here.astype(jnp.float32), axis=-1))
        dprob = jnp.einsum('jqhd,jkhd->jhqk', grad_here, value_near)
        probs = weights / total
        dscore = bfloat_round(probs * (dprob - jnp.transpose(delta, (0, 2, 1))[..., None]))
        probs_round = bfloat_round(probs)
        query_part = jnp.einsum('jhqk,jkhd->jqhd', dscore, key_near) * scale
        query_grad_here = query_part.astype(jnp.bfloat16)
        key_entries = jnp.einsum('jhqk,jqhd->jkhd', dscore, query_here) * scale
        value_entries = jnp.einsum('jhqk,jqhd->jkhd', probs_round, grad_here)
        key_part = jax.ops.segment_sum(key_entries.reshape(BLK * NBR, BS, H, HD), flat, NB)
        value_part = jax.ops.segment_sum(value_entries.reshape(BLK * NBR, BS, H, HD), flat, NB)
        remote = (block_owner != group)[:, None, None, None]
        key_part = jnp.where(remote, bfloat_round(key_part), key_part)
        value_part = jnp.where(remote, bfloat_round(value_part), value_part)
        return ((key_sum + key_part, value_sum + value_part), (attended_here, query_grad_here))
    start = (jnp.zeros((NB, BS, H, HD), jnp.float32), jnp.zeros((NB, BS, H, HD), jnp.float32))
    (key_sum, value_sum), (attended, query_grad) = lax.scan(one_group, start, jnp.arange(N_RES, dtype=jnp.int32))
    return (attended.reshape(N, width), query_grad.reshape(N, width), key_sum.astype(jnp.bfloat16).reshape(N, width), value_sum.astype(jnp.bfloat16).reshape(N, width))
```

```python
import functools
import math

import jax
import jax.numpy as jnp
from jax import lax
from jax.experimental import pallas as pl
from jax.experimental.pallas import tpu as pltpu
from jax.sharding import Mesh, PartitionSpec as P

HD = 128
BS = 128
NBR = 16
HALF = 64
NX, NYH, NYL, NC, NZ = 4, 2, 2, 2, 4
SLOTS = 6
META = 16
ROWS = 3 * 64 + META
NB = 64
QB = 16
SCALE = 1.0 / math.sqrt(HD)
LOG2E = math.log2(math.e)
CHIPS = ("x", "yh", "yl", "z")
VMEM = pl.BlockSpec(memory_space=pltpu.VMEM)
SMEM = pl.BlockSpec(memory_space=pltpu.SMEM)
PARAMS = pltpu.CompilerParams(vmem_limit_bytes=56 * 1024 * 1024)
F32 = jnp.float32
BF16 = jnp.bfloat16


def chip_index(x, yh, yl, z):
    return ((x * NYH + yh) * NYL + yl) * NZ + z


def working_chips():
    for x in range(SLOTS // NYH):
        for yh in range(NYH):
            for z in range(NZ):
                yield x, yh, z, z * SLOTS + x * NYH + yh


def pack_kernel(q_ref, k_ref, v_ref, lists_ref, rows_ref):
    x = pl.program_id(0)

    @pl.when(x < SLOTS // NYH)
    def _():
        for yh in range(NYH):
            for z in range(NZ):
                start = pl.multiple_of((z * SLOTS + x * NYH + yh) * HD, HD)
                for t, ref in enumerate((q_ref, k_ref, v_ref)):
                    piece = ref[:, pl.ds(start, HD)]
                    for yl in range(NYL):
                        dest = chip_index(0, yh, yl, z)
                        rows_ref[dest, t * HALF : (t + 1) * HALF] = piece

    @pl.when(x >= SLOTS // NYH)
    def _():
        rows_ref[:, : 3 * HALF] = jnp.zeros((NB // NX, 3 * HALF, HD), BF16)

    lists = lists_ref[...]
    for dest in range(NB // NX):
        rows_ref[dest, 3 * HALF :] = lists


def pack_grad_kernel(g_ref, grad_ref):
    for s in range(SLOTS):
        grad_ref[s] = g_ref[:, s * HD : (s + 1) * HD]
    grad_ref[SLOTS:] = jnp.zeros((NX * NYH - SLOTS, 2 * BS, HD), BF16)


def dot(a, b):
    return jnp.dot(a, b, preferred_element_type=F32)


def attention_kernel(
    info_ref,
    lists_ref,
    bias_ref,
    rows_ref,
    other_ref,
    grad_ref,
    att_ref,
    dq_ref,
    own_ref,
    far_ref,
    kv,
    kt,
    vt,
    mask,
    work,
    wide,
    dkv,
):
    core = info_ref[0]
    low = info_ref[1]
    bias = bias_ref[info_ref[2]] * LOG2E

    def fill(quad, _):
        for base, ref, at in ((0, rows_ref, HALF), (NB // 2, other_ref, 0)):
            lines = ref[quad * 4, at + 2 * HALF :].astype(F32)
            for half in range(2):
                src = quad * 4 + half * 2
                slot = base + quad * 2 + half
                k_block = jnp.concatenate(
                    [ref[src, at : at + HALF], ref[src + 1, at : at + HALF]], axis=0
                )
                v_at = at + HALF
                v_block = jnp.concatenate(
                    [ref[src, v_at : v_at + HALF], ref[src + 1, v_at : v_at + HALF]], axis=0
                )
                kv[slot] = jnp.concatenate([k_block, v_block], axis=1)
                kt[slot] = k_block.T
                vt[slot] = v_block.T
                dkv[slot] = jnp.zeros((BS, 2 * HD), F32)
                shown = jnp.where(lines[half : half + 1] == 1.0, 0.0, -jnp.inf)
                mask[slot] = jnp.broadcast_to(shown, (BS, BS)).T
        return 0

    lax.fori_loop(0, NB // 4, fill, 0)

    def diagonal(a, b):
        zero = jnp.zeros((HD, HD), BF16)
        return jnp.concatenate(
            [jnp.concatenate([a, zero], axis=1), jnp.concatenate([zero, b], axis=1)], axis=0
        )

    def one_block(i, _):
        pair = i // 2
        half = i % 2
        quad = pair * 2 + low
        src = quad * 4 + half * 2
        q = jnp.concatenate([rows_ref[src, :HALF], rows_ref[src + 1, :HALF]], axis=0)
        g = grad_ref[i]
        gt = g.T
        into = diagonal(q.T, gt)
        out_of = diagonal(q, g)
        line = quad * 4 + 2 + half
        chain = lists_ref[line, NBR]
        slots = []
        shifts = []
        for j in range(NBR):
            n = lists_ref[line, j]
            far = ((n // 2) % 2 != core).astype(jnp.int32)
            other_line = far * NB + (n // 4) * 4 + 2 + n % 2
            slots.append(far * (NB // 2) + (n // 4) * 2 + n % 2)
            shifts.append(jnp.where(lists_ref[other_line, NBR] != chain, bias, 0.0))
        peak = jnp.full((8, BS), -jnp.inf, F32)
        for j in range(NBR):
            both = dot(kv[slots[j]], into)
            score = both[:, :BS] * (SCALE * LOG2E) + (mask[slots[j]] + shifts[j])
            work[j] = score
            wide[j] = both[:, BS:]
            peak = jnp.maximum(peak, jnp.max(score.reshape(BS // 8, 8, BS), axis=0))
        peak = jnp.max(peak, axis=0, keepdims=True)
        total = jnp.zeros((8, BS), F32)
        mixed = jnp.zeros((HD, BS), F32)
        for j in range(0, NBR, 2):
            pair_weights = []
            for u in (j, j + 1):
                weights = jnp.exp2(work[u] - peak)
                work[u] = weights
                total = total + jnp.sum(weights.reshape(BS // 8, 8, BS), axis=0)
                pair_weights.append(weights.astype(BF16))
            vt_pair = jnp.concatenate([vt[slots[j]], vt[slots[j + 1]]], axis=1)
            mixed = mixed + dot(vt_pair, jnp.concatenate(pair_weights, axis=0))
        total = jnp.sum(total, axis=0, keepdims=True)
        attended = (mixed / total).astype(BF16)
        att_ref[i] = attended.T
        delta = jnp.sum(gt.astype(F32) * attended.astype(F32), axis=0, keepdims=True)
        inverse = 1.0 / total
        dqt = jnp.zeros((HD, BS), F32)
        for j in range(0, NBR, 2):
            pair_scores = []
            for u in (j, j + 1):
                probs = work[u] * inverse
                dscore = (probs * (wide[u] - delta)).astype(BF16)
                pair_scores.append(dscore)
                dkv[slots[u]] += dot(
                    jnp.concatenate([dscore, probs.astype(BF16)], axis=1), out_of
                )
            kt_pair = jnp.concatenate([kt[slots[j]], kt[slots[j + 1]]], axis=1)
            dqt = dqt + dot(kt_pair, jnp.concatenate(pair_scores, axis=0))
        dq = (dqt * SCALE).astype(BF16).T
        for yl in range(NYL):
            dest = (pair * 2 + yl) * 4 + half * 2
            dq_ref[dest] = dq[:HALF]
            dq_ref[dest + 1] = dq[HALF:]
        return 0

    lax.fori_loop(0, QB, one_block, 0)

    def drain(b, _):
        src = b * 2
        for t, scale in enumerate((SCALE, 1.0)):
            near = dkv[b, :, t * HD : (t + 1) * HD] * scale
            far = (dkv[NB // 2 + b, :, t * HD : (t + 1) * HD] * scale).astype(BF16)
            for h in range(2):
                own_ref[src + h, t] = near[h * HALF : (h + 1) * HALF]
                far_ref[src + h, t] = far[h * HALF : (h + 1) * HALF]
        return 0

    lax.fori_loop(0, NB // 2, drain, 0)


def merge_kernel(dq_ref, own_ref, came_ref, out_ref):
    out_ref[:, :HALF] = dq_ref[...]
    for t in range(2):
        both = own_ref[:, t] + came_ref[:, t].astype(F32)
        out_ref[:, (t + 1) * HALF : (t + 2) * HALF] = both.astype(BF16)


def unpack_kernel(info_ref, rows_ref, dq_ref, dk_ref, dv_ref):
    low = info_ref[1]
    for x, yh, z, head in working_chips():
        lane = slice(head * HD, (head + 1) * HD)
        zero = chip_index(x, yh, 0, z)
        one = chip_index(x, yh, 1, z)
        dq_ref[:, lane] = rows_ref[zero + low * NZ, :HALF]
        for t, ref in ((1, dk_ref), (2, dv_ref)):
            part = slice(t * HALF, (t + 1) * HALF)
            both = rows_ref[zero, part].astype(F32) + rows_ref[one, part].astype(F32)
            ref[:, lane] = both.astype(BF16)


def join_kernel(att_ref, out_ref):
    for s in range(SLOTS):
        out_ref[:, s * HD : (s + 1) * HD] = att_ref[s]


def shape(dims, dtype):
    return jax.ShapeDtypeStruct(dims, dtype)


def body(queries, keys, values, out_grad, chain_bias, chain_of_block, key_valid, neighbours):
    swap = [(0, 1), (1, 0)]
    core = lax.axis_index("c")
    low = lax.axis_index("yl")
    slot = jnp.minimum(lax.axis_index("x") * NYH + lax.axis_index("yh"), SLOTS - 1)
    info = jnp.stack([core, low, slot, slot]).astype(jnp.int32)

    lists = jnp.concatenate([neighbours, chain_of_block[:, None]], axis=1)
    lists = jnp.concatenate([key_valid.reshape(2, BS), jnp.pad(lists, ((0, 0), (0, BS - 1 - NBR)))])
    lists = jnp.pad(lists, ((0, META - 4), (0, 0))).astype(BF16)

    whole = pl.BlockSpec((HALF, NZ * SLOTS * HD), lambda x: (0, 0))
    rows = pl.pallas_call(
        pack_kernel,
        grid=(NX,),
        out_shape=shape((NB, ROWS, HD), BF16),
        in_specs=[whole, whole, whole, pl.BlockSpec((META, BS), lambda x: (0, 0))],
        out_specs=pl.BlockSpec((NB // NX, ROWS, HD), lambda x: (x, 0, 0)),
        compiler_params=PARAMS,
        name="pack",
    )(queries, keys, values, lists)
    grads = pl.pallas_call(
        pack_grad_kernel,
        out_shape=shape((NX * NYH, 2 * BS, HD), BF16),
        in_specs=[VMEM],
        out_specs=VMEM,
        compiler_params=PARAMS,
        name="pack_grad",
    )(out_grad)

    rows = lax.all_to_all(rows, CHIPS, split_axis=0, concat_axis=0, tiled=True)
    other = lax.ppermute(rows[:, HALF:], "c", swap)
    grads = lax.all_to_all(grads, ("x", "yh"), split_axis=0, concat_axis=0, tiled=True)
    lists = jnp.stack(
        [
            rows.reshape(NB // NZ, NZ, ROWS, HD)[:, 0, 3 * HALF : 3 * HALF + 4],
            other.reshape(NB // NZ, NZ, ROWS - HALF, HD)[:, 0, 2 * HALF : 2 * HALF + 4],
        ]
    )
    lists = lists.astype(jnp.int32).reshape(2 * NB, HD)

    table = pltpu.VMEM((NB, BS, HD), BF16)
    att, dq, own, far = pl.pallas_call(
        attention_kernel,
        out_shape=(
            shape((QB, BS, HD), BF16),
            shape((NB, HALF, HD), BF16),
            shape((NB, 2, HALF, HD), F32),
            shape((NB, 2, HALF, HD), BF16),
        ),
        in_specs=[SMEM, SMEM, SMEM, VMEM, VMEM, VMEM],
        out_specs=(VMEM,) * 4,
        scratch_shapes=[
            pltpu.VMEM((NB, BS, 2 * HD), BF16),
            table,
            table,
            pltpu.VMEM((NB, BS, BS), F32),
            pltpu.VMEM((NBR, BS, BS), F32),
            pltpu.VMEM((NBR, BS, BS), F32),
            pltpu.VMEM((NB, BS, 2 * HD), F32),
        ],
        compiler_params=PARAMS,
        name="attention",
    )(info, lists, chain_bias, rows, other, grads.reshape(QB, BS, HD))

    came = lax.ppermute(far, "c", swap)
    att = lax.all_to_all(
        att.reshape(NX * NYH, 2 * BS, HD), ("x", "yh"), split_axis=0, concat_axis=0, tiled=True
    )
    attended = pl.pallas_call(
        join_kernel,
        out_shape=shape((2 * BS, SLOTS * HD), BF16),
        in_specs=[VMEM],
        out_specs=VMEM,
        compiler_params=PARAMS,
        name="join",
    )(att)
    steps = 8
    each = NB // steps
    split = pl.BlockSpec((each, 2, HALF, HD), lambda i: (i, 0, 0, 0))
    back = pl.pallas_call(
        merge_kernel,
        grid=(steps,),
        out_shape=shape((NB, 3 * HALF, HD), BF16),
        in_specs=[pl.BlockSpec((each, HALF, HD), lambda i: (i, 0, 0)), split, split],
        out_specs=pl.BlockSpec((each, 3 * HALF, HD), lambda i: (i, 0, 0)),
        compiler_params=PARAMS,
        name="merge",
    )(dq, own, came)
    back = lax.all_to_all(back, CHIPS, split_axis=0, concat_axis=0, tiled=True)
    flat = shape((HALF, NZ * SLOTS * HD), BF16)
    dq, dk, dv = pl.pallas_call(
        unpack_kernel,
        out_shape=(flat, flat, flat),
        in_specs=[SMEM, VMEM],
        out_specs=(VMEM,) * 3,
        compiler_params=PARAMS,
        name="unpack",
    )(info, back)
    return attended, dq, dk, dv


def solution(mesh):
    grid = Mesh(mesh.devices.reshape(NX, NYH, NYL, NC, NZ), ("x", "yh", "yl", "c", "z"))
    res = ("x", "yh", "yl", "c")
    both = P(res + ("z",), None)
    return jax.shard_map(
        body,
        mesh=grid,
        in_specs=(both, both, both, P(res, "z"), P("z"), P(res), P(res), P(res, None)),
        out_specs=(P(res, "z"), both, both, both),
        check_vma=False,
    )
```

```python
import functools
import math

import jax
import jax.numpy as jnp
from jax import lax
from jax.experimental import pallas as pl
from jax.experimental.pallas import tpu as pltpu
from jax.sharding import Mesh, PartitionSpec as P

HD = 128
BS = 128
NBR = 16
HALF = 64
QUARTER = 32
NX, NYH, NYL, NC, NZ = 4, 2, 2, 2, 4
SLOTS = 6
META = 16
SIDES = NX * NYH
Q_AT = 2 * HALF + META
ROWS = Q_AT + QUARTER
BACK = 2 * HALF + QUARTER
NB = 64
QB = 16
SCALE = 1.0 / math.sqrt(HD)
LOG2E = math.log2(math.e)
CHIPS = ("x", "yh", "yl", "z")
PARTS = 4
ANY = pl.BlockSpec(memory_space=pl.ANY)
VMEM = pl.BlockSpec(memory_space=pltpu.VMEM)
SMEM = pl.BlockSpec(memory_space=pltpu.SMEM)
PARAMS = pltpu.CompilerParams(vmem_limit_bytes=50 * 1024 * 1024)
FULL = pltpu.CompilerParams(vmem_limit_bytes=62 * 1024 * 1024)
F32 = jnp.float32
BF16 = jnp.bfloat16


def chip_index(x, yh, yl, z):
    return ((x * NYH + yh) * NYL + yl) * NZ + z


def pack_kernel(info_ref, chain_ref, q_ref, k_ref, v_ref, valid_ref, near_ref, rows_ref, lists):
    x = pl.program_id(0)
    low = info_ref[1]

    @pl.when(x == 0)
    def _():
        lane = lax.broadcasted_iota(jnp.int32, (1, BS), 1)
        lists[...] = jnp.zeros((META, BS), F32)
        lists[0:2] = valid_ref[...].astype(F32)
        lists[2:4, 0:NBR] = near_ref[...].astype(F32)
        for half in range(2):
            line = lists[2 + half : 3 + half]
            chain = jnp.full((1, BS), chain_ref[half], jnp.int32).astype(F32)
            lists[2 + half : 3 + half] = jnp.where(lane == NBR, chain, line)

    @pl.when(x < SLOTS // NYH)
    def _():
        for yh in range(NYH):
            for z in range(NZ):
                start = pl.multiple_of((z * SLOTS + x * NYH + yh) * HD, HD)
                first, second = chip_index(0, yh, 0, z), chip_index(0, yh, 1, z)
                for t, ref in enumerate((k_ref, v_ref)):
                    piece = ref[:, pl.ds(start, HD)]
                    for dest in (first, second):
                        rows_ref[dest, t * HALF : (t + 1) * HALF] = piece
                query = q_ref[:, pl.ds(start, HD)]
                upper, lower = query[:QUARTER], query[QUARTER:]
                rows_ref[first, Q_AT:] = jnp.where(low == 0, upper, lower)
                rows_ref[second, Q_AT:] = jnp.where(low == 0, lower, upper)

    @pl.when(x >= SLOTS // NYH)
    def _():
        rows_ref[...] = jnp.zeros((NB // NX, ROWS, HD), BF16)

    held = lists[...].astype(BF16)
    for dest in range(NB // NX):
        rows_ref[dest, 2 * HALF : Q_AT] = held


def pack_grad_kernel(info_ref, g_ref, keep_ref, swap_ref):
    x, yh = info_ref[2], info_ref[3]
    for d in range(NX):
        first = jnp.minimum(x ^ d, SLOTS // NYH - 1) * NYH
        for ref, side in ((keep_ref, yh), (swap_ref, 1 - yh)):
            start = pl.multiple_of((first + side) * HD, HD)
            ref[d] = g_ref[:, pl.ds(start, HD)]


def dot(a, b):
    return jnp.dot(a, b, preferred_element_type=F32)


def attention_kernel(
    info_ref,
    lists_ref,
    bias_ref,
    rows_hbm,
    other_hbm,
    lower_hbm,
    grad_keep_hbm,
    grad_came_hbm,
    grad_1_hbm,
    grad_2_hbm,
    grad_3_hbm,
    att_keep_hbm,
    att_swap_hbm,
    back_hbm,
    far_hbm,
    lower_out_hbm,
    *refs,
):
    (
        rows_ref,
        other_ref,
        lower_ref,
        lower_out_ref,
        grad_ref,
        att_ref,
        kv,
        kt,
        vt,
        mask,
        scores,
        weights,
        dprob_even,
        dprob_odd,
        stats,
        dkv,
        back_ref,
        far_ref,
        rows_sem,
        other_sem,
        lower_sem,
        grad_sem,
        att_sem,
        back_sem,
        far_sem,
    ) = refs
    core = info_ref[0]
    low = info_ref[1]
    x, yh = info_ref[2], info_ref[3]
    slot_here = x * NYH + yh
    dprob = (dprob_even, dprob_odd)
    bias = bias_ref[jnp.minimum(slot_here, SLOTS - 1)] * LOG2E
    part = NB // PARTS

    def chunk(k):
        return pl.ds(k * part, part)

    def copies(source, target, sems, lines):
        return [
            pltpu.make_async_copy(
                source.at[chunk(k), pl.ds(0, lines)], target.at[chunk(k)], sems.at[k]
            )
            for k in range(PARTS)
        ]

    rows_in = copies(rows_hbm, rows_ref, rows_sem, ROWS)
    other_in = copies(other_hbm, other_ref, other_sem, Q_AT)
    grad_pieces = [(grad_keep_hbm.at[0], grad_came_hbm.at[0])]
    for ref in (grad_1_hbm, grad_2_hbm, grad_3_hbm):
        grad_pieces.append((ref.at[0], ref.at[1]))
    grads_in = []
    att_out = []
    for d, pieces in enumerate(grad_pieces):
        for n, (piece, side, att_hbm) in enumerate(
            ((pieces[0], yh, att_keep_hbm), (pieces[1], 1 - yh, att_swap_hbm))
        ):
            pair = (x ^ d) * NYH + side
            at = d * 2 + n
            grads_in.append(pltpu.make_async_copy(piece, grad_ref.at[pair], grad_sem.at[at]))
            att_out.append(pltpu.make_async_copy(att_ref.at[pair], att_hbm.at[d], att_sem.at[at]))
    lower_in = pltpu.make_async_copy(lower_hbm, lower_ref, lower_sem.at[0])
    lower_out = pltpu.make_async_copy(lower_out_ref, lower_out_hbm, lower_sem.at[1])
    for copy in rows_in + other_in + [lower_in] + grads_in:
        copy.start()

    def grad_block(i):
        start = pl.multiple_of((i % 2) * BS, BS)
        return grad_ref[i // 2, pl.ds(start, BS)]

    def fill(quad, base, ref):
        lines = ref[quad * 4, 2 * HALF : Q_AT].astype(F32)
        for half in range(2):
            src = quad * 4 + half * 2
            slot = base + quad * 2 + half
            k_block = jnp.concatenate([ref[src, :HALF], ref[src + 1, :HALF]], axis=0)
            v_block = jnp.concatenate(
                [ref[src, HALF : 2 * HALF], ref[src + 1, HALF : 2 * HALF]], axis=0
            )
            kv[slot] = jnp.concatenate([k_block, v_block], axis=1)
            kt[slot] = k_block.T
            vt[slot] = v_block.T
            dkv[slot] = jnp.zeros((BS, 2 * HD), F32)
            shown = jnp.where(lines[half : half + 1] == 1.0, 0.0, -jnp.inf)
            mask[slot] = jnp.broadcast_to(shown, (BS, BS)).T

    for base, ref, waits in ((0, rows_ref, rows_in), (NB // 2, other_ref, other_in)):
        for k, copy in enumerate(waits):
            copy.wait()

            def fill_one(m, _, base=base, ref=ref, k=k):
                fill(k * (part // 4) + m, base, ref)
                return 0

            lax.fori_loop(0, part // 4, fill_one, 0)
    lower_in.wait()
    for copy in grads_in:
        copy.wait()

    def diagonal(a, b):
        zero = jnp.zeros((HD, HD), BF16)
        return jnp.concatenate(
            [jnp.concatenate([a, zero], axis=1), jnp.concatenate([zero, b], axis=1)], axis=0
        )

    def place(i):
        pair = i // 2
        half = i % 2
        quad = pair * 2 + low
        return pair, half, quad

    def query_block(i):
        pair, half, quad = place(i)
        src = quad * 4 + half * 2
        low_src = pair * 4 + half * 2
        pieces = []
        for h in range(2):
            pieces += [rows_ref[src + h, Q_AT:], lower_ref[low_src + h]]
        return jnp.concatenate(pieces, axis=0)

    def listed(i, j):
        _, half, quad = place(i)
        n = lists_ref[quad * 4 + 2 + half, j]
        far = ((n // 2) % 2 != core).astype(jnp.int32)
        line = far * NB + (n // 4) * 4 + 2 + n % 2
        return far * (NB // 2) + (n // 4) * 2 + n % 2, line

    class Scores:
        def __init__(self, i, parity):
            _, half, quad = place(i)
            self.i = i
            self.chain = lists_ref[quad * 4 + 2 + half, NBR]
            self.into = diagonal(query_block(i).T, grad_block(i).T)
            self.dprob = dprob[parity]
            self.peak = jnp.full((8, BS), -jnp.inf, F32)

        def step(self, j):
            slot, line = listed(self.i, j)
            shift = jnp.where(lists_ref[line, NBR] != self.chain, bias, 0.0)
            both = dot(kv[slot], self.into)
            score = both[:, :BS] * (SCALE * LOG2E) + (mask[slot] + shift)
            scores[j] = score
            self.dprob[j] = both[:, BS:]
            self.peak = jnp.maximum(self.peak, jnp.max(score.reshape(BS // 8, 8, BS), axis=0))

        def end(self):
            stats[0:1] = jnp.max(self.peak, axis=0, keepdims=True)

    class Mix:
        def __init__(self, i):
            self.i = i
            self.peak = stats[0:1]
            self.total = jnp.zeros((8, BS), F32)
            self.mixed = jnp.zeros((HD, BS), F32)
            self.held = []

        def step(self, j):
            row = jnp.exp2(scores[j] - self.peak)
            weights[j] = row
            self.total = self.total + jnp.sum(row.reshape(BS // 8, 8, BS), axis=0)
            self.held.append((row.astype(BF16), vt[listed(self.i, j)[0]]))
            if j % 2:
                (r0, v0), (r1, v1) = self.held
                self.held = []
                self.mixed = self.mixed + dot(
                    jnp.concatenate([v0, v1], axis=1), jnp.concatenate([r0, r1], axis=0)
                )

        def end(self):
            total = jnp.sum(self.total, axis=0, keepdims=True)
            attended = (self.mixed / total).astype(BF16)
            pair, half, _ = place(self.i)
            att_ref[pair, pl.ds(pl.multiple_of(half * BS, BS), BS)] = attended.T
            grad = grad_block(self.i).T.astype(F32)
            stats[1:2] = jnp.sum(grad * attended.astype(F32), axis=0, keepdims=True)
            stats[2:3] = 1.0 / total

    class Back:
        def __init__(self, i, parity):
            self.i = i
            self.dprob = dprob[parity]
            self.delta = stats[1:2]
            self.inverse = stats[2:3]
            self.out_of = diagonal(query_block(i), grad_block(i))
            self.dqt = jnp.zeros((HD, BS), F32)
            self.held = []

        def step(self, j):
            slot, _ = listed(self.i, j)
            probs = weights[j] * self.inverse
            dscore = (probs * (self.dprob[j] - self.delta)).astype(BF16)
            both = jnp.concatenate([dscore, probs.astype(BF16)], axis=1)
            dkv[slot] += dot(both, self.out_of)
            self.held.append((dscore, kt[slot]))
            if j % 2:
                (s0, k0), (s1, k1) = self.held
                self.held = []
                self.dqt = self.dqt + dot(
                    jnp.concatenate([k0, k1], axis=1), jnp.concatenate([s0, s1], axis=0)
                )

        def end(self):
            pair, half, quad = place(self.i)
            dq = (self.dqt * SCALE).astype(BF16).T
            for h in range(2):
                at = h * HALF
                back_ref[quad * 4 + half * 2 + h, 2 * HALF :] = dq[at : at + QUARTER]
                lower_out_ref[pair * 4 + half * 2 + h] = dq[at + QUARTER : at + HALF]

    def together(*stages):
        for j in range(NBR):
            for stage in stages:
                stage.step(j)
        for stage in stages:
            stage.end()

    together(Scores(0, 0))
    together(Mix(0), Scores(1, 1))

    def rounds(r, _):
        for parity in range(2):
            i = r * 2 + parity
            together(Back(i, parity), Mix(i + 1), Scores(i + 2, parity))
        return 0

    lax.fori_loop(0, QB // 2 - 1, rounds, 0)
    together(Back(QB - 2, 0), Mix(QB - 1))
    together(Back(QB - 1, 1))

    for copy in att_out + [lower_out]:
        copy.start()
    far_out = copies(far_ref, far_hbm, far_sem, 2 * HALF)
    back_out = copies(back_ref, back_hbm, back_sem, BACK)

    def drain(b, base, target):
        for t, scale in enumerate((SCALE, 1.0)):
            block = (dkv[base + b, :, t * HD : (t + 1) * HD] * scale).astype(BF16)
            rows = slice(t * HALF, (t + 1) * HALF)
            for h in range(2):
                target[b * 2 + h, rows] = block[h * HALF : (h + 1) * HALF]

    for base, target, outs in ((NB // 2, far_ref, far_out), (0, back_ref, back_out)):
        for k, copy in enumerate(outs):

            def drain_one(m, _, base=base, target=target, k=k):
                drain(k * (part // 2) + m, base, target)
                return 0

            lax.fori_loop(0, part // 2, drain_one, 0)
            copy.start()
    for copy in att_out + [lower_out] + far_out + back_out:
        copy.wait()


def merge_kernel(
    info_ref,
    back_hbm,
    came_hbm,
    lower_hbm,
    out_hbm,
    back_ref,
    came_ref,
    back_sem,
    came_sem,
    out_sem,
    lower_sem,
):
    other = 1 - info_ref[1]
    each = NB // PARTS
    near = slice(0, 2 * HALF)
    copies = []
    for k in range(PARTS):
        part = pl.ds(k * each, each)
        copies.append(
            (
                pltpu.make_async_copy(
                    back_hbm.at[part, near], back_ref.at[part], back_sem.at[k]
                ),
                pltpu.make_async_copy(came_hbm.at[part], came_ref.at[part], came_sem.at[k]),
                pltpu.make_async_copy(back_ref.at[part], out_hbm.at[part, near], out_sem.at[k]),
            )
        )
    lower = []
    for n in range(SIDES):
        target = out_hbm.at[pl.ds((n * 2 + other) * NZ, NZ), slice(2 * HALF, BACK)]
        source = lower_hbm.at[pl.ds(n * NZ, NZ)]
        lower.append(pltpu.make_async_copy(source, target, lower_sem.at[n]))
    for mine, came, _ in copies:
        mine.start()
        came.start()
    for copy in lower:
        copy.start()
    for k, (mine, came, out) in enumerate(copies):
        mine.wait()
        came.wait()

        def add(m, _, k=k):
            n = k * each + m
            back_ref[n] = (back_ref[n].astype(F32) + came_ref[n].astype(F32)).astype(BF16)
            return 0

        lax.fori_loop(0, each, add, 0, unroll=4)
        out.start()
    for _, _, out in copies:
        out.wait()
    for copy in lower:
        copy.wait()


def unpack_kernel(info_ref, rows_hbm, dq_ref, dk_ref, dv_ref, rows_ref, sems):
    low = info_ref[1]
    each = NB // NX
    copies = [
        pltpu.make_async_copy(
            rows_hbm.at[pl.ds(x * each, each)], rows_ref.at[pl.ds(x * each, each)], sems.at[x]
        )
        for x in range(SLOTS // NYH)
    ]
    for copy in copies:
        copy.start()
    for x, copy in enumerate(copies):
        copy.wait()
        for yh in range(NYH):
            for z in range(NZ):
                head = z * SLOTS + x * NYH + yh
                lane = slice(head * HD, (head + 1) * HD)
                zero = chip_index(x, yh, 0, z)
                one = chip_index(x, yh, 1, z)
                dq_ref[:QUARTER, lane] = rows_ref[zero + low * NZ, 2 * HALF :]
                dq_ref[QUARTER:, lane] = rows_ref[zero + (1 - low) * NZ, 2 * HALF :]
                for t, ref in enumerate((dk_ref, dv_ref)):
                    part = slice(t * HALF, (t + 1) * HALF)
                    both = rows_ref[zero, part].astype(F32) + rows_ref[one, part].astype(F32)
                    ref[:, lane] = both.astype(BF16)


def join_kernel(info_ref, keep_hbm, came_hbm, one_hbm, two_hbm, three_hbm, out_hbm, sems):
    x, yh = info_ref[2], info_ref[3]
    pieces = [(keep_hbm.at[0], came_hbm.at[0])]
    for ref in (one_hbm, two_hbm, three_hbm):
        pieces.append((ref.at[0], ref.at[1]))

    def each(act):
        for d, pair in enumerate(pieces):
            first = (x ^ d) * NYH

            @pl.when(first < SLOTS)
            def _(d=d, pair=pair, first=first):
                for n, side in enumerate((yh, 1 - yh)):
                    lane = pl.ds(pl.multiple_of((first + side) * HD, HD), HD)
                    act(pltpu.make_async_copy(pair[n], out_hbm.at[:, lane], sems.at[d * 2 + n]))

    each(lambda copy: copy.start())
    each(lambda copy: copy.wait())


def shape(dims, dtype):
    return jax.ShapeDtypeStruct(dims, dtype)


def attend(*operands):
    four = shape((NX, 2 * BS, HD), BF16)
    table = pltpu.VMEM((NB, BS, HD), BF16)
    near = pltpu.VMEM((NBR, BS, BS), F32)
    sems = pltpu.SemaphoreType.DMA((PARTS,))
    return pl.pallas_call(
        attention_kernel,
        out_shape=(
            four,
            four,
            shape((NB, BACK, HD), BF16),
            shape((NB, 2 * HALF, HD), BF16),
            shape((SIDES * NZ, QUARTER, HD), BF16),
        ),
        in_specs=[SMEM, SMEM, SMEM] + [ANY] * 8,
        out_specs=(ANY,) * 5,
        scratch_shapes=[
            pltpu.VMEM((NB, ROWS, HD), BF16),
            pltpu.VMEM((NB, Q_AT, HD), BF16),
            pltpu.VMEM((SIDES * NZ, QUARTER, HD), BF16),
            pltpu.VMEM((SIDES * NZ, QUARTER, HD), BF16),
            pltpu.VMEM((SIDES, 2 * BS, HD), BF16),
            pltpu.VMEM((SIDES, 2 * BS, HD), BF16),
            pltpu.VMEM((NB, BS, 2 * HD), BF16),
            table,
            table,
            pltpu.VMEM((NB, BS, BS), F32),
            near,
            near,
            near,
            near,
            pltpu.VMEM((8, BS), F32),
            pltpu.VMEM((NB, BS, 2 * HD), F32),
            pltpu.VMEM((NB, BACK, HD), BF16),
            pltpu.VMEM((NB, 2 * HALF, HD), BF16),
            sems,
            sems,
            pltpu.SemaphoreType.DMA((2,)),
            pltpu.SemaphoreType.DMA((SIDES,)),
            pltpu.SemaphoreType.DMA((SIDES,)),
            sems,
            sems,
        ],
        compiler_params=PARAMS,
        name="attention",
    )(*operands)


def body(queries, keys, values, out_grad, chain_bias, chain_of_block, key_valid, neighbours):
    swap = [(0, 1), (1, 0)]
    info = jnp.stack([lax.axis_index(name) for name in ("c", "yl", "x", "yh")]).astype(jnp.int32)

    whole = pl.BlockSpec((HALF, NZ * SLOTS * HD), lambda x: (0, 0))
    packed = pl.pallas_call(
        pack_kernel,
        grid=(NX,),
        out_shape=shape((NB, ROWS, HD), BF16),
        in_specs=[
            SMEM,
            SMEM,
            whole,
            whole,
            whole,
            pl.BlockSpec((2, BS), lambda x: (0, 0)),
            pl.BlockSpec((2, NBR), lambda x: (0, 0)),
        ],
        out_specs=pl.BlockSpec((NB // NX, ROWS, HD), lambda x: (x, 0, 0)),
        scratch_shapes=[pltpu.VMEM((META, BS), F32)],
        compiler_params=FULL,
        name="pack",
    )(info, chain_of_block, queries, keys, values, key_valid.reshape(2, BS), neighbours)
    four = shape((NX, 2 * BS, HD), BF16)
    keep, sent = pl.pallas_call(
        pack_grad_kernel,
        out_shape=(four, four),
        in_specs=[SMEM, VMEM],
        out_specs=(VMEM, VMEM),
        compiler_params=FULL,
        name="pack_grad",
    )(info, out_grad)

    def along_x(kept, came, onward):
        moved = []
        for d in range(1, NX):
            pairs = [(i, i ^ d) for i in range(NX) if (i ^ d if onward else i) < SLOTS // NYH]
            moved.append(lax.ppermute(jnp.stack([kept[d], came[d]]), "x", pairs))
        return moved

    came = lax.ppermute(sent, "yh", swap)
    packed, keep, came = lax.optimization_barrier((packed, keep, came))
    rows = lax.all_to_all(packed, CHIPS, split_axis=0, concat_axis=0, tiled=True)
    grads = along_x(keep, came, True)
    rows, grads = lax.optimization_barrier((rows, grads))
    grads = [keep, came] + grads
    other = lax.ppermute(rows, "c", swap)
    theirs = lax.dynamic_index_in_dim(
        rows.reshape(SIDES, NYL, NZ, ROWS, HD)[:, :, :, Q_AT:],
        1 - lax.axis_index("yl"),
        axis=1,
        keepdims=False,
    )
    lower = lax.ppermute(theirs.reshape(SIDES * NZ, QUARTER, HD), "yl", swap)
    lists = jnp.stack(
        [
            rows.reshape(NB // NZ, NZ, ROWS, HD)[:, 0, 2 * HALF : 2 * HALF + 4],
            other.reshape(NB // NZ, NZ, ROWS, HD)[:, 0, 2 * HALF : 2 * HALF + 4],
        ]
    )
    lists = lists.astype(jnp.int32).reshape(2 * NB, HD)

    att_keep, att_swap, back, far, lower = attend(info, lists, chain_bias, rows, other, lower, *grads)

    came = lax.ppermute(far, "c", swap)
    lower_came = lax.ppermute(lower, "yl", swap)
    att_came = lax.ppermute(att_swap, "yh", swap)
    sems = pltpu.SemaphoreType.DMA((PARTS,))
    back = pl.pallas_call(
        merge_kernel,
        out_shape=shape((NB, BACK, HD), BF16),
        in_specs=[SMEM, ANY, ANY, ANY],
        out_specs=ANY,
        scratch_shapes=[
            pltpu.VMEM((NB, 2 * HALF, HD), BF16),
            pltpu.VMEM((NB, 2 * HALF, HD), BF16),
            sems,
            sems,
            sems,
            pltpu.SemaphoreType.DMA((SIDES,)),
        ],
        input_output_aliases={1: 0},
        compiler_params=PARAMS,
        name="merge",
    )(info, back, came, lower_came)
    back, att_keep, att_came = lax.optimization_barrier((back, att_keep, att_came))
    back = lax.all_to_all(back, CHIPS, split_axis=0, concat_axis=0, tiled=True)
    moved = along_x(att_keep, att_came, False)
    attended = pl.pallas_call(
        join_kernel,
        out_shape=shape((2 * BS, SLOTS * HD), BF16),
        in_specs=[SMEM] + [ANY] * 5,
        out_specs=ANY,
        scratch_shapes=[pltpu.SemaphoreType.DMA((SIDES,))],
        compiler_params=PARAMS,
        name="join",
    )(info, att_keep, att_came, *moved)
    flat = shape((HALF, NZ * SLOTS * HD), BF16)
    dq, dk, dv = pl.pallas_call(
        unpack_kernel,
        out_shape=(flat, flat, flat),
        in_specs=[SMEM, ANY],
        out_specs=(VMEM,) * 3,
        scratch_shapes=[
            pltpu.VMEM((NB, BACK, HD), BF16),
            pltpu.SemaphoreType.DMA((SLOTS // NYH,)),
        ],
        compiler_params=PARAMS,
        name="unpack",
    )(info, back)
    return attended, dq, dk, dv


def solution(mesh):
    grid = Mesh(mesh.devices.reshape(NX, NYH, NYL, NC, NZ), ("x", "yh", "yl", "c", "z"))
    res = ("x", "yh", "yl", "c")
    both = P(res + ("z",), None)
    return jax.shard_map(
        body,
        mesh=grid,
        in_specs=(both, both, both, P(res, "z"), P("z"), P(res), P(res), P(res, None)),
        out_specs=(P(res, "z"), both, both, both),
        check_vma=False,
    )
```

```python
import functools
import math

import jax
import jax.numpy as jnp
from jax import lax
from jax.experimental import pallas as pl
from jax.experimental.pallas import tpu as pltpu
from jax.sharding import Mesh, PartitionSpec as P

HD = 128
BS = 128
NBR = 16
HALF = 64
QUARTER = 32
NX, NYH, NYL, NC, NZ = 4, 2, 2, 2, 4
SLOTS = 6
META = 16
SIDES = NX * NYH
Q_AT = 2 * HALF + META
ROWS = Q_AT + QUARTER
BACK = 2 * HALF + QUARTER
NB = 64
QB = 16
SCALE = 1.0 / math.sqrt(HD)
LOG2E = math.log2(math.e)
CHIPS = ("x", "yh", "yl", "z")
PARTS = 4
ANY = pl.BlockSpec(memory_space=pl.ANY)
VMEM = pl.BlockSpec(memory_space=pltpu.VMEM)
SMEM = pl.BlockSpec(memory_space=pltpu.SMEM)
PARAMS = pltpu.CompilerParams(vmem_limit_bytes=50 * 1024 * 1024)
FULL = pltpu.CompilerParams(vmem_limit_bytes=62 * 1024 * 1024)
F32 = jnp.float32
BF16 = jnp.bfloat16


def chip_index(x, yh, yl, z):
    return ((x * NYH + yh) * NYL + yl) * NZ + z


def pack_kernel(info_ref, chain_ref, q_ref, k_ref, v_ref, valid_ref, near_ref, rows_ref, lists):
    x = pl.program_id(0)
    low = info_ref[1]

    @pl.when(x == 0)
    def _():
        lane = lax.broadcasted_iota(jnp.int32, (1, BS), 1)
        lists[...] = jnp.zeros((META, BS), F32)
        lists[0:2] = valid_ref[...].astype(F32)
        lists[2:4, 0:NBR] = near_ref[...].astype(F32)
        for half in range(2):
            line = lists[2 + half : 3 + half]
            chain = jnp.full((1, BS), chain_ref[half], jnp.int32).astype(F32)
            lists[2 + half : 3 + half] = jnp.where(lane == NBR, chain, line)

    @pl.when(x < SLOTS // NYH)
    def _():
        for yh in range(NYH):
            for z in range(NZ):
                start = pl.multiple_of((z * SLOTS + x * NYH + yh) * HD, HD)
                first, second = chip_index(0, yh, 0, z), chip_index(0, yh, 1, z)
                for t, ref in enumerate((k_ref, v_ref)):
                    piece = ref[:, pl.ds(start, HD)]
                    for dest in (first, second):
                        rows_ref[dest, t * HALF : (t + 1) * HALF] = piece
                query = q_ref[:, pl.ds(start, HD)]
                upper, lower = query[:QUARTER], query[QUARTER:]
                rows_ref[first, Q_AT:] = jnp.where(low == 0, upper, lower)
                rows_ref[second, Q_AT:] = jnp.where(low == 0, lower, upper)

    @pl.when(x >= SLOTS // NYH)
    def _():
        rows_ref[...] = jnp.zeros((NB // NX, ROWS, HD), BF16)

    held = lists[...].astype(BF16)
    for dest in range(NB // NX):
        rows_ref[dest, 2 * HALF : Q_AT] = held


def pack_grad_kernel(info_ref, g_ref, *grad_refs):
    x, yh = info_ref[2], info_ref[3]
    for d, ref in enumerate(grad_refs):
        first = jnp.minimum(x ^ d, SLOTS // NYH - 1) * NYH
        for n, side in enumerate((yh, 1 - yh)):
            ref[n] = g_ref[:, pl.ds(pl.multiple_of((first + side) * HD, HD), HD)]


def dot(a, b):
    return jnp.dot(a, b, preferred_element_type=F32)


def attention_kernel(
    info_ref,
    near_ref,
    lists_ref,
    bias_ref,
    rows_hbm,
    other_hbm,
    lower_hbm,
    grad_came_hbm,
    grad_0_hbm,
    grad_1_hbm,
    grad_2_hbm,
    grad_3_hbm,
    att_keep_hbm,
    att_swap_hbm,
    back_hbm,
    far_hbm,
    lower_out_hbm,
    *refs,
):
    (
        rows_ref,
        other_ref,
        lower_ref,
        lower_out_ref,
        grad_ref,
        att_ref,
        kv,
        kt,
        vt,
        mask,
        scores,
        weights,
        dprob_even,
        dprob_odd,
        stats,
        dkv,
        back_ref,
        far_ref,
        rows_sem,
        other_sem,
        lower_sem,
        grad_sem,
        att_sem,
        back_sem,
        far_sem,
    ) = refs
    core = info_ref[0]
    low = info_ref[1]
    x, yh = info_ref[2], info_ref[3]
    slot_here = x * NYH + yh
    dprob = (dprob_even, dprob_odd)
    bias = bias_ref[jnp.minimum(slot_here, SLOTS - 1)] * LOG2E
    part = NB // PARTS

    def chunk(k):
        return pl.ds(k * part, part)

    def copies(source, target, sems, lines):
        return [
            pltpu.make_async_copy(
                source.at[chunk(k), pl.ds(0, lines)], target.at[chunk(k)], sems.at[k]
            )
            for k in range(PARTS)
        ]

    rows_in = copies(rows_hbm, rows_ref, rows_sem, ROWS)
    other_in = copies(other_hbm, other_ref, other_sem, Q_AT)
    grad_pieces = []
    for d, ref in enumerate((grad_0_hbm, grad_1_hbm, grad_2_hbm, grad_3_hbm)):
        grad_pieces.append((ref.at[0], grad_came_hbm.at[d]))
    grads_in = []
    att_out = []
    for d, pieces in enumerate(grad_pieces):
        for n, (piece, side, att_hbm) in enumerate(
            ((pieces[0], yh, att_keep_hbm), (pieces[1], 1 - yh, att_swap_hbm))
        ):
            pair = (x ^ d) * NYH + side
            at = d * 2 + n
            grads_in.append(pltpu.make_async_copy(piece, grad_ref.at[pair], grad_sem.at[at]))
            att_out.append(pltpu.make_async_copy(att_ref.at[pair], att_hbm.at[d], att_sem.at[at]))
    lower_in = pltpu.make_async_copy(lower_hbm, lower_ref, lower_sem.at[0])
    lower_out = pltpu.make_async_copy(lower_out_ref, lower_out_hbm, lower_sem.at[1])
    for copy in rows_in + other_in + [lower_in] + grads_in:
        copy.start()

    def grad_block(i):
        start = pl.multiple_of((i % 2) * BS, BS)
        return grad_ref[i // 2, pl.ds(start, BS)]

    def fill(quad, base, ref):
        lines = ref[quad * 4, 2 * HALF : Q_AT].astype(F32)
        for half in range(2):
            src = quad * 4 + half * 2
            slot = base + quad * 2 + half
            k_block = jnp.concatenate([ref[src, :HALF], ref[src + 1, :HALF]], axis=0)
            v_block = jnp.concatenate(
                [ref[src, HALF : 2 * HALF], ref[src + 1, HALF : 2 * HALF]], axis=0
            )
            kv[slot] = jnp.concatenate([k_block, v_block], axis=1)
            kt[slot] = k_block.T
            vt[slot] = v_block.T
            dkv[slot] = jnp.zeros((BS, 2 * HD), F32)
            shown = jnp.where(lines[half : half + 1] == 1.0, 0.0, -jnp.inf)
            mask[slot] = jnp.broadcast_to(shown, (BS, BS)).T

    for base, ref, waits in ((0, rows_ref, rows_in), (NB // 2, other_ref, other_in)):
        for k, copy in enumerate(waits):
            copy.wait()

            def fill_one(m, _, base=base, ref=ref, k=k):
                fill(k * (part // 4) + m, base, ref)
                return 0

            lax.fori_loop(0, part // 4, fill_one, 0, unroll=2)
    lower_in.wait()
    for copy in grads_in:
        copy.wait()

    def diagonal(a, b):
        zero = jnp.zeros((HD, HD), BF16)
        return jnp.concatenate(
            [jnp.concatenate([a, zero], axis=1), jnp.concatenate([zero, b], axis=1)], axis=0
        )

    def place(i):
        pair = i // 2
        half = i % 2
        quad = pair * 2 + low
        return pair, half, quad

    def query_block(i):
        pair, half, quad = place(i)
        src = quad * 4 + half * 2
        low_src = pair * 4 + half * 2
        pieces = []
        for h in range(2):
            pieces += [rows_ref[src + h, Q_AT:], lower_ref[low_src + h]]
        return jnp.concatenate(pieces, axis=0)

    def listed(i, j):
        _, half, quad = place(i)
        return near_ref[quad * 2 + half, j]

    def chain_at(i, j):
        _, half, quad = place(i)
        return lists_ref[near_ref[quad * 2 + half, NBR + j], NBR]

    class Scores:
        def __init__(self, i, parity):
            _, half, quad = place(i)
            self.i = i
            self.chain = lists_ref[quad * 4 + 2 + half, NBR]
            self.into = diagonal(query_block(i).T, grad_block(i).T)
            self.dprob = dprob[parity]
            self.peak = jnp.full((8, BS), -jnp.inf, F32)

        def step(self, j):
            slot = listed(self.i, j)
            shift = jnp.where(chain_at(self.i, j) != self.chain, bias, 0.0)
            both = dot(kv[slot], self.into)
            score = both[:, :BS] * (SCALE * LOG2E) + (mask[slot] + shift)
            scores[j] = score
            self.dprob[j] = both[:, BS:]
            self.peak = jnp.maximum(self.peak, jnp.max(score.reshape(BS // 8, 8, BS), axis=0))

        def end(self):
            stats[0:1] = jnp.max(self.peak, axis=0, keepdims=True)

    class Mix:
        def __init__(self, i):
            self.i = i
            self.peak = stats[0:1]
            self.total = jnp.zeros((8, BS), F32)
            self.mixed = jnp.zeros((HD, BS), F32)
            self.held = []

        def step(self, j):
            row = jnp.exp2(scores[j] - self.peak)
            weights[j] = row
            self.total = self.total + jnp.sum(row.reshape(BS // 8, 8, BS), axis=0)
            self.held.append((row.astype(BF16), vt[listed(self.i, j)]))
            if j % 2:
                (r0, v0), (r1, v1) = self.held
                self.held = []
                self.mixed = self.mixed + dot(
                    jnp.concatenate([v0, v1], axis=1), jnp.concatenate([r0, r1], axis=0)
                )

        def end(self):
            total = jnp.sum(self.total, axis=0, keepdims=True)
            attended = (self.mixed / total).astype(BF16)
            pair, half, _ = place(self.i)
            att_ref[pair, pl.ds(pl.multiple_of(half * BS, BS), BS)] = attended.T
            grad = grad_block(self.i).T.astype(F32)
            stats[1:2] = jnp.sum(grad * attended.astype(F32), axis=0, keepdims=True)
            stats[2:3] = 1.0 / total

    class Back:
        def __init__(self, i, parity):
            self.i = i
            self.dprob = dprob[parity]
            self.delta = stats[1:2]
            self.inverse = stats[2:3]
            self.out_of = diagonal(query_block(i), grad_block(i))
            self.dqt = jnp.zeros((HD, BS), F32)
            self.held = []

        def step(self, j):
            slot = listed(self.i, j)
            probs = weights[j] * self.inverse
            dscore = (probs * (self.dprob[j] - self.delta)).astype(BF16)
            both = jnp.concatenate([dscore, probs.astype(BF16)], axis=1)
            dkv[slot] += dot(both, self.out_of)
            self.held.append((dscore, kt[slot]))
            if j % 2:
                (s0, k0), (s1, k1) = self.held
                self.held = []
                self.dqt = self.dqt + dot(
                    jnp.concatenate([k0, k1], axis=1), jnp.concatenate([s0, s1], axis=0)
                )

        def end(self):
            pair, half, quad = place(self.i)
            dq = (self.dqt * SCALE).astype(BF16).T
            for h in range(2):
                at = h * HALF
                back_ref[quad * 4 + half * 2 + h, 2 * HALF :] = dq[at : at + QUARTER]
                lower_out_ref[pair * 4 + half * 2 + h] = dq[at + QUARTER : at + HALF]

    def together(*stages):
        for j in range(NBR):
            for stage in stages:
                stage.step(j)
        for stage in stages:
            stage.end()

    together(Scores(0, 0))
    together(Mix(0), Scores(1, 1))

    def rounds(r, _):
        for parity in range(2):
            i = r * 2 + parity
            together(Back(i, parity), Mix(i + 1), Scores(i + 2, parity))
        return 0

    lax.fori_loop(0, QB // 2 - 1, rounds, 0)
    together(Back(QB - 2, 0), Mix(QB - 1))
    together(Back(QB - 1, 1))

    for copy in att_out + [lower_out]:
        copy.start()
    far_out = copies(far_ref, far_hbm, far_sem, 2 * HALF)
    back_out = copies(back_ref, back_hbm, back_sem, BACK)

    def drain(b, base, target):
        for t, scale in enumerate((SCALE, 1.0)):
            block = (dkv[base + b, :, t * HD : (t + 1) * HD] * scale).astype(BF16)
            rows = slice(t * HALF, (t + 1) * HALF)
            for h in range(2):
                target[b * 2 + h, rows] = block[h * HALF : (h + 1) * HALF]

    for base, target, outs in ((NB // 2, far_ref, far_out), (0, back_ref, back_out)):
        for k, copy in enumerate(outs):

            def drain_one(m, _, base=base, target=target, k=k):
                drain(k * (part // 2) + m, base, target)
                return 0

            lax.fori_loop(0, part // 2, drain_one, 0)
            copy.start()
    for copy in att_out + [lower_out] + far_out + back_out:
        copy.wait()


def merge_kernel(
    info_ref,
    back_hbm,
    came_hbm,
    lower_hbm,
    out_hbm,
    back_ref,
    came_ref,
    back_sem,
    came_sem,
    out_sem,
    lower_sem,
):
    other = 1 - info_ref[1]
    each = NB // PARTS
    near = slice(0, 2 * HALF)
    copies = []
    for k in range(PARTS):
        part = pl.ds(k * each, each)
        copies.append(
            (
                pltpu.make_async_copy(
                    back_hbm.at[part, near], back_ref.at[part], back_sem.at[k]
                ),
                pltpu.make_async_copy(came_hbm.at[part], came_ref.at[part], came_sem.at[k]),
                pltpu.make_async_copy(back_ref.at[part], out_hbm.at[part, near], out_sem.at[k]),
            )
        )
    lower = []
    for n in range(SIDES):
        target = out_hbm.at[pl.ds((n * 2 + other) * NZ, NZ), slice(2 * HALF, BACK)]
        source = lower_hbm.at[pl.ds(n * NZ, NZ)]
        lower.append(pltpu.make_async_copy(source, target, lower_sem.at[n]))
    for mine, came, _ in copies:
        mine.start()
        came.start()
    for copy in lower:
        copy.start()
    for k, (mine, came, out) in enumerate(copies):
        mine.wait()
        came.wait()

        def add(m, _, k=k):
            n = k * each + m
            back_ref[n] = (back_ref[n].astype(F32) + came_ref[n].astype(F32)).astype(BF16)
            return 0

        lax.fori_loop(0, each, add, 0, unroll=4)
        out.start()
    for _, _, out in copies:
        out.wait()
    for copy in lower:
        copy.wait()


def join(info_ref, pieces, out_hbm, sems, act):
    x, yh = info_ref[2], info_ref[3]
    for d, pair in enumerate(pieces):
        first = (x ^ d) * NYH

        @pl.when(first < SLOTS)
        def _(d=d, pair=pair, first=first):
            for n, side in enumerate((yh, 1 - yh)):
                lane = pl.ds(pl.multiple_of((first + side) * HD, HD), HD)
                act(pltpu.make_async_copy(pair[n], out_hbm.at[:, lane], sems.at[d * 2 + n]))


def unpack_kernel(
    info_ref,
    rows_hbm,
    keep_hbm,
    came_hbm,
    one_hbm,
    two_hbm,
    three_hbm,
    dq_ref,
    dk_ref,
    dv_ref,
    att_hbm,
    rows_ref,
    sems,
    att_sems,
):
    pieces = [(keep_hbm.at[0], came_hbm.at[0])]
    for ref in (one_hbm, two_hbm, three_hbm):
        pieces.append((ref.at[0], ref.at[1]))
    join(info_ref, pieces, att_hbm, att_sems, lambda copy: copy.start())
    low = info_ref[1]
    each = NB // NX
    copies = [
        pltpu.make_async_copy(
            rows_hbm.at[pl.ds(x * each, each)], rows_ref.at[pl.ds(x * each, each)], sems.at[x]
        )
        for x in range(SLOTS // NYH)
    ]
    for copy in copies:
        copy.start()
    for x, copy in enumerate(copies):
        copy.wait()
        for yh in range(NYH):
            for z in range(NZ):
                head = z * SLOTS + x * NYH + yh
                lane = slice(head * HD, (head + 1) * HD)
                zero = chip_index(x, yh, 0, z)
                one = chip_index(x, yh, 1, z)
                dq_ref[:QUARTER, lane] = rows_ref[zero + low * NZ, 2 * HALF :]
                dq_ref[QUARTER:, lane] = rows_ref[zero + (1 - low) * NZ, 2 * HALF :]
                for t, ref in enumerate((dk_ref, dv_ref)):
                    part = slice(t * HALF, (t + 1) * HALF)
                    both = rows_ref[zero, part].astype(F32) + rows_ref[one, part].astype(F32)
                    ref[:, lane] = both.astype(BF16)
    join(info_ref, pieces, att_hbm, att_sems, lambda copy: copy.wait())


def shape(dims, dtype):
    return jax.ShapeDtypeStruct(dims, dtype)


def attend(*operands):
    four = shape((NX, 2 * BS, HD), BF16)
    table = pltpu.VMEM((NB, BS, HD), BF16)
    near = pltpu.VMEM((NBR, BS, BS), F32)
    sems = pltpu.SemaphoreType.DMA((PARTS,))
    return pl.pallas_call(
        attention_kernel,
        out_shape=(
            four,
            four,
            shape((NB, BACK, HD), BF16),
            shape((NB, 2 * HALF, HD), BF16),
            shape((SIDES * NZ, QUARTER, HD), BF16),
        ),
        in_specs=[SMEM] * 4 + [ANY] * 8,
        out_specs=(ANY,) * 5,
        scratch_shapes=[
            pltpu.VMEM((NB, ROWS, HD), BF16),
            pltpu.VMEM((NB, Q_AT, HD), BF16),
            pltpu.VMEM((SIDES * NZ, QUARTER, HD), BF16),
            pltpu.VMEM((SIDES * NZ, QUARTER, HD), BF16),
            pltpu.VMEM((SIDES, 2 * BS, HD), BF16),
            pltpu.VMEM((SIDES, 2 * BS, HD), BF16),
            pltpu.VMEM((NB, BS, 2 * HD), BF16),
            table,
            table,
            pltpu.VMEM((NB, BS, BS), F32),
            near,
            near,
            near,
            near,
            pltpu.VMEM((8, BS), F32),
            pltpu.VMEM((NB, BS, 2 * HD), F32),
            pltpu.VMEM((NB, BACK, HD), BF16),
            pltpu.VMEM((NB, 2 * HALF, HD), BF16),
            sems,
            sems,
            pltpu.SemaphoreType.DMA((2,)),
            pltpu.SemaphoreType.DMA((SIDES,)),
            pltpu.SemaphoreType.DMA((SIDES,)),
            sems,
            sems,
        ],
        compiler_params=PARAMS,
        name="attention",
    )(*operands)


def body(queries, keys, values, out_grad, chain_bias, chain_of_block, key_valid, neighbours):
    swap = [(0, 1), (1, 0)]
    info = jnp.stack([lax.axis_index(name) for name in ("c", "yl", "x", "yh")]).astype(jnp.int32)

    whole = pl.BlockSpec((HALF, NZ * SLOTS * HD), lambda x: (0, 0))
    packed = pl.pallas_call(
        pack_kernel,
        grid=(NX,),
        out_shape=shape((NB, ROWS, HD), BF16),
        in_specs=[
            SMEM,
            SMEM,
            whole,
            whole,
            whole,
            pl.BlockSpec((2, BS), lambda x: (0, 0)),
            pl.BlockSpec((2, NBR), lambda x: (0, 0)),
        ],
        out_specs=pl.BlockSpec((NB // NX, ROWS, HD), lambda x: (x, 0, 0)),
        scratch_shapes=[pltpu.VMEM((META, BS), F32)],
        compiler_params=FULL,
        name="pack",
    )(info, chain_of_block, queries, keys, values, key_valid.reshape(2, BS), neighbours)
    packed, out_grad = lax.optimization_barrier((packed, out_grad))
    rows = lax.all_to_all(packed, CHIPS, split_axis=0, concat_axis=0, tiled=True)
    grads = pl.pallas_call(
        pack_grad_kernel,
        out_shape=(shape((2, 2 * BS, HD), BF16),) * NX,
        in_specs=[SMEM, VMEM],
        out_specs=(VMEM,) * NX,
        compiler_params=FULL,
        name="pack_grad",
    )(info, out_grad)

    def along_x(pieces, onward):
        moved = []
        for d, piece in enumerate(pieces, 1):
            pairs = [(i, i ^ d) for i in range(NX) if (i ^ d if onward else i) < SLOTS // NYH]
            moved.append(lax.ppermute(piece, "x", pairs))
        return moved

    moved = along_x(grads[1:], True)
    rows, moved = lax.optimization_barrier((rows, moved))
    grads = [grads[0]] + moved
    came = lax.ppermute(jnp.stack([piece[1] for piece in grads]), "yh", swap)
    grads = [came] + grads
    other = lax.ppermute(rows, "c", swap)
    theirs = lax.dynamic_index_in_dim(
        rows.reshape(SIDES, NYL, NZ, ROWS, HD)[:, :, :, Q_AT:],
        1 - lax.axis_index("yl"),
        axis=1,
        keepdims=False,
    )
    lower = lax.ppermute(theirs.reshape(SIDES * NZ, QUARTER, HD), "yl", swap)
    mine = rows.reshape(NB // NZ, NZ, ROWS, HD)[:, 0, 2 * HALF : 2 * HALF + 4]
    far = other.reshape(NB // NZ, NZ, ROWS, HD)[:, 0, 2 * HALF : 2 * HALF + 4]
    lists = jnp.stack([mine, far]).astype(jnp.int32).reshape(2 * NB, HD)
    block = mine[:, 2:, :NBR].astype(jnp.int32)
    away = (block // 2 % 2 != lax.axis_index("c")).astype(jnp.int32)
    there = block // 4
    slots = away * (NB // 2) + there * 2 + block % 2
    lines = away * NB + there * 4 + 2 + block % 2
    near = jnp.concatenate([slots, lines], axis=-1).reshape(NB // 2, 2 * NBR)
    att_keep, att_swap, back, far, lower = attend(info, near, lists, chain_bias, rows, other, lower, *grads)

    came = lax.ppermute(far, "c", swap)
    lower_came = lax.ppermute(lower, "yl", swap)
    att_came = lax.ppermute(att_swap, "yh", swap)
    sems = pltpu.SemaphoreType.DMA((PARTS,))
    back = pl.pallas_call(
        merge_kernel,
        out_shape=shape((NB, BACK, HD), BF16),
        in_specs=[SMEM, ANY, ANY, ANY],
        out_specs=ANY,
        scratch_shapes=[
            pltpu.VMEM((NB, 2 * HALF, HD), BF16),
            pltpu.VMEM((NB, 2 * HALF, HD), BF16),
            sems,
            sems,
            sems,
            pltpu.SemaphoreType.DMA((SIDES,)),
        ],
        input_output_aliases={1: 0},
        compiler_params=PARAMS,
        name="merge",
    )(info, back, came, lower_came)
    back, att_keep, att_came = lax.optimization_barrier((back, att_keep, att_came))
    back = lax.all_to_all(back, CHIPS, split_axis=0, concat_axis=0, tiled=True)
    moved = along_x([jnp.stack([att_keep[d], att_came[d]]) for d in range(1, NX)], False)
    flat = shape((HALF, NZ * SLOTS * HD), BF16)
    dq, dk, dv, attended = pl.pallas_call(
        unpack_kernel,
        out_shape=(flat, flat, flat, shape((2 * BS, SLOTS * HD), BF16)),
        in_specs=[SMEM] + [ANY] * 6,
        out_specs=(VMEM, VMEM, VMEM, ANY),
        scratch_shapes=[
            pltpu.VMEM((NB, BACK, HD), BF16),
            pltpu.SemaphoreType.DMA((SLOTS // NYH,)),
            pltpu.SemaphoreType.DMA((SIDES,)),
        ],
        compiler_params=PARAMS,
        name="unpack",
    )(info, back, att_keep, att_came, *moved)
    return attended, dq, dk, dv


def solution(mesh):
    grid = Mesh(mesh.devices.reshape(NX, NYH, NYL, NC, NZ), ("x", "yh", "yl", "c", "z"))
    res = ("x", "yh", "yl", "c")
    both = P(res + ("z",), None)
    return jax.shard_map(
        body,
        mesh=grid,
        in_specs=(both, both, both, P(res, "z"), P("z"), P(res), P(res), P(res, None)),
        out_specs=(P(res, "z"), both, both, both),
        check_vma=False,
    )
```

```python
import functools
import math

import jax
import jax.numpy as jnp
from jax import lax
from jax.experimental import pallas as pl
from jax.experimental.pallas import tpu as pltpu
from jax.sharding import Mesh, PartitionSpec as P

HD = 128
BS = 128
NBR = 16
HALF = 64
QUARTER = 32
NX, NYH, NYL, NC, NZ = 4, 2, 2, 2, 4
SLOTS = 6
META = 16
SIDES = NX * NYH
Q_AT = 2 * HALF + META
ROWS = Q_AT + QUARTER
BACK = 2 * HALF + QUARTER
NB = 64
QB = 16
SCALE = 1.0 / math.sqrt(HD)
LOG2E = math.log2(math.e)
CHIPS = ("x", "yh", "yl", "z")
PARTS = 8
ANY = pl.BlockSpec(memory_space=pl.ANY)
VMEM = pl.BlockSpec(memory_space=pltpu.VMEM)
SMEM = pl.BlockSpec(memory_space=pltpu.SMEM)
PARAMS = pltpu.CompilerParams(vmem_limit_bytes=50 * 1024 * 1024)
FULL = pltpu.CompilerParams(vmem_limit_bytes=62 * 1024 * 1024)
F32 = jnp.float32
BF16 = jnp.bfloat16


def chip_index(x, yh, yl, z):
    return ((x * NYH + yh) * NYL + yl) * NZ + z


def pack_kernel(info_ref, chain_ref, q_ref, k_ref, v_ref, valid_ref, near_ref, rows_ref, lists):
    x = pl.program_id(0)
    low = info_ref[1]

    @pl.when(x == 0)
    def _():
        lane = lax.broadcasted_iota(jnp.int32, (1, BS), 1)
        lists[...] = jnp.zeros((META, BS), F32)
        lists[0:2] = valid_ref[...].astype(F32)
        lists[2:4, 0:NBR] = near_ref[...].astype(F32)
        for half in range(2):
            line = lists[2 + half : 3 + half]
            chain = jnp.full((1, BS), chain_ref[half], jnp.int32).astype(F32)
            lists[2 + half : 3 + half] = jnp.where(lane == NBR, chain, line)

    @pl.when(x < SLOTS // NYH)
    def _():
        for yh in range(NYH):
            for z in range(NZ):
                start = pl.multiple_of((z * SLOTS + x * NYH + yh) * HD, HD)
                first, second = chip_index(0, yh, 0, z), chip_index(0, yh, 1, z)
                for t, ref in enumerate((k_ref, v_ref)):
                    piece = ref[:, pl.ds(start, HD)]
                    for dest in (first, second):
                        rows_ref[dest, t * HALF : (t + 1) * HALF] = piece
                query = q_ref[:, pl.ds(start, HD)]
                upper, lower = query[:QUARTER], query[QUARTER:]
                rows_ref[first, Q_AT:] = jnp.where(low == 0, upper, lower)
                rows_ref[second, Q_AT:] = jnp.where(low == 0, lower, upper)

    @pl.when(x >= SLOTS // NYH)
    def _():
        rows_ref[...] = jnp.zeros((NB // NX, ROWS, HD), BF16)

    held = lists[...].astype(BF16)
    for dest in range(NB // NX):
        rows_ref[dest, 2 * HALF : Q_AT] = held


def pack_grad_kernel(info_ref, g_ref, *grad_refs):
    x, yh = info_ref[2], info_ref[3]
    for d, ref in enumerate(grad_refs):
        first = jnp.minimum(x ^ d, SLOTS // NYH - 1) * NYH
        for n, side in enumerate((yh, 1 - yh)):
            ref[n] = g_ref[:, pl.ds(pl.multiple_of((first + side) * HD, HD), HD)]


def dot(a, b):
    return jnp.dot(a, b, preferred_element_type=F32)


def attention_kernel(
    info_ref,
    near_ref,
    lists_ref,
    bias_ref,
    rows_hbm,
    other_hbm,
    lower_hbm,
    grad_came_hbm,
    grad_0_hbm,
    grad_1_hbm,
    grad_2_hbm,
    grad_3_hbm,
    att_keep_hbm,
    att_swap_hbm,
    back_hbm,
    far_hbm,
    lower_out_hbm,
    *refs,
):
    (
        rows_ref,
        other_ref,
        lower_ref,
        lower_out_ref,
        grad_ref,
        att_ref,
        kv,
        kt,
        vt,
        mask,
        scores,
        weights,
        dprob_even,
        dprob_odd,
        stats,
        dkv,
        back_ref,
        far_ref,
        rows_sem,
        other_sem,
        lower_sem,
        grad_sem,
        att_sem,
        back_sem,
        far_sem,
    ) = refs
    core = info_ref[0]
    low = info_ref[1]
    x, yh = info_ref[2], info_ref[3]
    slot_here = x * NYH + yh
    dprob = (dprob_even, dprob_odd)
    bias = bias_ref[jnp.minimum(slot_here, SLOTS - 1)] * LOG2E
    part = NB // PARTS

    def chunk(k):
        return pl.ds(k * part, part)

    def copies(source, target, sems, lines):
        return [
            pltpu.make_async_copy(
                source.at[chunk(k), pl.ds(0, lines)], target.at[chunk(k)], sems.at[k]
            )
            for k in range(PARTS)
        ]

    rows_in = copies(rows_hbm, rows_ref, rows_sem, ROWS)
    other_in = copies(other_hbm, other_ref, other_sem, Q_AT)
    grad_pieces = []
    for d, ref in enumerate((grad_0_hbm, grad_1_hbm, grad_2_hbm, grad_3_hbm)):
        grad_pieces.append((ref.at[0], grad_came_hbm.at[d]))
    grads_in = []
    att_out = []
    for d, pieces in enumerate(grad_pieces):
        for n, (piece, side, att_hbm) in enumerate(
            ((pieces[0], yh, att_keep_hbm), (pieces[1], 1 - yh, att_swap_hbm))
        ):
            pair = (x ^ d) * NYH + side
            at = d * 2 + n
            grads_in.append(pltpu.make_async_copy(piece, grad_ref.at[pair], grad_sem.at[at]))
            att_out.append(pltpu.make_async_copy(att_ref.at[pair], att_hbm.at[d], att_sem.at[at]))
    lower_in = pltpu.make_async_copy(lower_hbm, lower_ref, lower_sem.at[0])
    lower_out = pltpu.make_async_copy(lower_out_ref, lower_out_hbm, lower_sem.at[1])
    for copy in rows_in + other_in + [lower_in] + grads_in:
        copy.start()

    def grad_block(i):
        start = pl.multiple_of((i % 2) * BS, BS)
        return grad_ref[i // 2, pl.ds(start, BS)]

    def fill(quad, base, ref):
        lines = ref[quad * 4, 2 * HALF : Q_AT].astype(F32)
        for half in range(2):
            src = quad * 4 + half * 2
            slot = base + quad * 2 + half
            k_block = jnp.concatenate([ref[src, :HALF], ref[src + 1, :HALF]], axis=0)
            v_block = jnp.concatenate(
                [ref[src, HALF : 2 * HALF], ref[src + 1, HALF : 2 * HALF]], axis=0
            )
            kv[slot] = jnp.concatenate([k_block, v_block], axis=1)
            kt[slot] = k_block.T
            vt[slot] = v_block.T
            dkv[slot] = jnp.zeros((BS, 2 * HD), F32)
            shown = jnp.where(lines[half : half + 1] == 1.0, 0.0, -jnp.inf)
            mask[slot] = jnp.broadcast_to(shown, (BS, BS)).T

    for base, ref, waits in ((0, rows_ref, rows_in), (NB // 2, other_ref, other_in)):
        for k, copy in enumerate(waits):
            copy.wait()

            def fill_one(m, _, base=base, ref=ref, k=k):
                fill(k * (part // 4) + m, base, ref)
                return 0

            lax.fori_loop(0, part // 4, fill_one, 0, unroll=2)
    lower_in.wait()
    for copy in grads_in:
        copy.wait()

    def diagonal(a, b):
        zero = jnp.zeros((HD, HD), BF16)
        return jnp.concatenate(
            [jnp.concatenate([a, zero], axis=1), jnp.concatenate([zero, b], axis=1)], axis=0
        )

    def place(i):
        pair = i // 2
        half = i % 2
        quad = pair * 2 + low
        return pair, half, quad

    def query_block(i):
        pair, half, quad = place(i)
        src = quad * 4 + half * 2
        low_src = pair * 4 + half * 2
        pieces = []
        for h in range(2):
            pieces += [rows_ref[src + h, Q_AT:], lower_ref[low_src + h]]
        return jnp.concatenate(pieces, axis=0)

    def listed(i, j):
        _, half, quad = place(i)
        return near_ref[quad * 2 + half, j]

    def chain_at(i, j):
        _, half, quad = place(i)
        return lists_ref[near_ref[quad * 2 + half, NBR + j], NBR]

    class Scores:
        def __init__(self, i, parity):
            _, half, quad = place(i)
            self.i = i
            self.chain = lists_ref[quad * 4 + 2 + half, NBR]
            self.into = diagonal(query_block(i).T, grad_block(i).T)
            self.dprob = dprob[parity]
            self.peak = jnp.full((8, BS), -jnp.inf, F32)

        def step(self, j):
            slot = listed(self.i, j)
            shift = jnp.where(chain_at(self.i, j) != self.chain, bias, 0.0)
            both = dot(kv[slot], self.into)
            score = both[:, :BS] * (SCALE * LOG2E) + (mask[slot] + shift)
            scores[j] = score
            self.dprob[j] = both[:, BS:]
            self.peak = jnp.maximum(self.peak, jnp.max(score.reshape(BS // 8, 8, BS), axis=0))

        def end(self):
            stats[0:1] = jnp.max(self.peak, axis=0, keepdims=True)

    class Mix:
        def __init__(self, i):
            self.i = i
            self.peak = stats[0:1]
            self.total = jnp.zeros((8, BS), F32)
            self.mixed = jnp.zeros((HD, BS), F32)
            self.held = []

        def step(self, j):
            row = jnp.exp2(scores[j] - self.peak)
            weights[j] = row
            self.total = self.total + jnp.sum(row.reshape(BS // 8, 8, BS), axis=0)
            self.held.append((row.astype(BF16), vt[listed(self.i, j)]))
            if j % 2:
                (r0, v0), (r1, v1) = self.held
                self.held = []
                self.mixed = self.mixed + dot(
                    jnp.concatenate([v0, v1], axis=1), jnp.concatenate([r0, r1], axis=0)
                )

        def end(self):
            total = jnp.sum(self.total, axis=0, keepdims=True)
            attended = (self.mixed / total).astype(BF16)
            pair, half, _ = place(self.i)
            att_ref[pair, pl.ds(pl.multiple_of(half * BS, BS), BS)] = attended.T
            grad = grad_block(self.i).T.astype(F32)
            stats[1:2] = jnp.sum(grad * attended.astype(F32), axis=0, keepdims=True)
            stats[2:3] = 1.0 / total

    class Back:
        def __init__(self, i, parity):
            self.i = i
            self.dprob = dprob[parity]
            self.delta = stats[1:2]
            self.inverse = stats[2:3]
            self.out_of = diagonal(query_block(i), grad_block(i))
            self.dqt = jnp.zeros((HD, BS), F32)
            self.held = []

        def step(self, j):
            slot = listed(self.i, j)
            probs = weights[j] * self.inverse
            dscore = (probs * (self.dprob[j] - self.delta)).astype(BF16)
            both = jnp.concatenate([dscore, probs.astype(BF16)], axis=1)
            dkv[slot] += dot(both, self.out_of)
            self.held.append((dscore, kt[slot]))
            if j % 2:
                (s0, k0), (s1, k1) = self.held
                self.held = []
                self.dqt = self.dqt + dot(
                    jnp.concatenate([k0, k1], axis=1), jnp.concatenate([s0, s1], axis=0)
                )

        def end(self):
            pair, half, quad = place(self.i)
            dq = (self.dqt * SCALE).astype(BF16).T
            for h in range(2):
                at = h * HALF
                back_ref[quad * 4 + half * 2 + h, 2 * HALF :] = dq[at : at + QUARTER]
                lower_out_ref[pair * 4 + half * 2 + h] = dq[at + QUARTER : at + HALF]

    def together(*stages):
        for j in range(NBR):
            for stage in stages:
                stage.step(j)
        for stage in stages:
            stage.end()

    together(Scores(0, 0))
    together(Mix(0), Scores(1, 1))

    def rounds(r, _):
        for parity in range(2):
            i = r * 2 + parity
            together(Back(i, parity), Mix(i + 1), Scores(i + 2, parity))
        return 0

    lax.fori_loop(0, QB // 2 - 1, rounds, 0)
    together(Back(QB - 2, 0), Mix(QB - 1))
    together(Back(QB - 1, 1))

    for copy in att_out + [lower_out]:
        copy.start()
    far_out = copies(far_ref, far_hbm, far_sem, 2 * HALF)
    back_out = copies(back_ref, back_hbm, back_sem, BACK)

    def drain(b, base, target):
        for t, scale in enumerate((SCALE, 1.0)):
            block = (dkv[base + b, :, t * HD : (t + 1) * HD] * scale).astype(BF16)
            rows = slice(t * HALF, (t + 1) * HALF)
            for h in range(2):
                target[b * 2 + h, rows] = block[h * HALF : (h + 1) * HALF]

    for base, target, outs in ((NB // 2, far_ref, far_out), (0, back_ref, back_out)):
        for k, copy in enumerate(outs):

            def drain_one(m, _, base=base, target=target, k=k):
                drain(k * (part // 2) + m, base, target)
                return 0

            lax.fori_loop(0, part // 2, drain_one, 0)
            copy.start()
    for copy in att_out + [lower_out] + far_out + back_out:
        copy.wait()


def merge_kernel(
    info_ref,
    back_hbm,
    came_hbm,
    lower_hbm,
    out_hbm,
    back_ref,
    came_ref,
    back_sem,
    came_sem,
    out_sem,
    lower_sem,
):
    other = 1 - info_ref[1]
    each = NB // PARTS
    near = slice(0, 2 * HALF)
    copies = []
    for k in range(PARTS):
        part = pl.ds(k * each, each)
        copies.append(
            (
                pltpu.make_async_copy(
                    back_hbm.at[part, near], back_ref.at[part], back_sem.at[k]
                ),
                pltpu.make_async_copy(came_hbm.at[part], came_ref.at[part], came_sem.at[k]),
                pltpu.make_async_copy(back_ref.at[part], out_hbm.at[part, near], out_sem.at[k]),
            )
        )
    lower = []
    for n in range(SIDES):
        target = out_hbm.at[pl.ds((n * 2 + other) * NZ, NZ), slice(2 * HALF, BACK)]
        source = lower_hbm.at[pl.ds(n * NZ, NZ)]
        lower.append(pltpu.make_async_copy(source, target, lower_sem.at[n]))
    for mine, came, _ in copies:
        mine.start()
        came.start()
    for copy in lower:
        copy.start()
    for k, (mine, came, out) in enumerate(copies):
        mine.wait()
        came.wait()

        def add(m, _, k=k):
            n = k * each + m
            back_ref[n] = (back_ref[n].astype(F32) + came_ref[n].astype(F32)).astype(BF16)
            return 0

        lax.fori_loop(0, each, add, 0, unroll=4)
        out.start()
    for _, _, out in copies:
        out.wait()
    for copy in lower:
        copy.wait()


def join(info_ref, pieces, out_hbm, sems, act):
    x, yh = info_ref[2], info_ref[3]
    for d, pair in enumerate(pieces):
        first = (x ^ d) * NYH

        @pl.when(first < SLOTS)
        def _(d=d, pair=pair, first=first):
            for n, side in enumerate((yh, 1 - yh)):
                lane = pl.ds(pl.multiple_of((first + side) * HD, HD), HD)
                act(pltpu.make_async_copy(pair[n], out_hbm.at[:, lane], sems.at[d * 2 + n]))


def unpack_kernel(
    info_ref,
    rows_hbm,
    keep_hbm,
    came_hbm,
    one_hbm,
    two_hbm,
    three_hbm,
    dq_ref,
    dk_ref,
    dv_ref,
    att_hbm,
    rows_ref,
    sems,
    att_sems,
):
    pieces = [(keep_hbm.at[0], came_hbm.at[0])]
    for ref in (one_hbm, two_hbm, three_hbm):
        pieces.append((ref.at[0], ref.at[1]))
    join(info_ref, pieces, att_hbm, att_sems, lambda copy: copy.start())
    low = info_ref[1]
    each = NB // NX
    copies = [
        pltpu.make_async_copy(
            rows_hbm.at[pl.ds(x * each, each)], rows_ref.at[pl.ds(x * each, each)], sems.at[x]
        )
        for x in range(SLOTS // NYH)
    ]
    for copy in copies:
        copy.start()
    for x, copy in enumerate(copies):
        copy.wait()
        for yh in range(NYH):
            for z in range(NZ):
                head = z * SLOTS + x * NYH + yh
                lane = slice(head * HD, (head + 1) * HD)
                zero = chip_index(x, yh, 0, z)
                one = chip_index(x, yh, 1, z)
                dq_ref[:QUARTER, lane] = rows_ref[zero + low * NZ, 2 * HALF :]
                dq_ref[QUARTER:, lane] = rows_ref[zero + (1 - low) * NZ, 2 * HALF :]
                for t, ref in enumerate((dk_ref, dv_ref)):
                    part = slice(t * HALF, (t + 1) * HALF)
                    both = rows_ref[zero, part].astype(F32) + rows_ref[one, part].astype(F32)
                    ref[:, lane] = both.astype(BF16)
    join(info_ref, pieces, att_hbm, att_sems, lambda copy: copy.wait())


def shape(dims, dtype):
    return jax.ShapeDtypeStruct(dims, dtype)


def attend(*operands):
    four = shape((NX, 2 * BS, HD), BF16)
    table = pltpu.VMEM((NB, BS, HD), BF16)
    near = pltpu.VMEM((NBR, BS, BS), F32)
    sems = pltpu.SemaphoreType.DMA((PARTS,))
    return pl.pallas_call(
        attention_kernel,
        out_shape=(
            four,
            four,
            shape((NB, BACK, HD), BF16),
            shape((NB, 2 * HALF, HD), BF16),
            shape((SIDES * NZ, QUARTER, HD), BF16),
        ),
        in_specs=[SMEM] * 4 + [ANY] * 8,
        out_specs=(ANY,) * 5,
        scratch_shapes=[
            pltpu.VMEM((NB, ROWS, HD), BF16),
            pltpu.VMEM((NB, Q_AT, HD), BF16),
            pltpu.VMEM((SIDES * NZ, QUARTER, HD), BF16),
            pltpu.VMEM((SIDES * NZ, QUARTER, HD), BF16),
            pltpu.VMEM((SIDES, 2 * BS, HD), BF16),
            pltpu.VMEM((SIDES, 2 * BS, HD), BF16),
            pltpu.VMEM((NB, BS, 2 * HD), BF16),
            table,
            table,
            pltpu.VMEM((NB, BS, BS), F32),
            near,
            near,
            near,
            near,
            pltpu.VMEM((8, BS), F32),
            pltpu.VMEM((NB, BS, 2 * HD), F32),
            pltpu.VMEM((NB, BACK, HD), BF16),
            pltpu.VMEM((NB, 2 * HALF, HD), BF16),
            sems,
            sems,
            pltpu.SemaphoreType.DMA((2,)),
            pltpu.SemaphoreType.DMA((SIDES,)),
            pltpu.SemaphoreType.DMA((SIDES,)),
            sems,
            sems,
        ],
        compiler_params=PARAMS,
        name="attention",
    )(*operands)


def body(queries, keys, values, out_grad, chain_bias, chain_of_block, key_valid, neighbours):
    swap = [(0, 1), (1, 0)]
    info = jnp.stack([lax.axis_index(name) for name in ("c", "yl", "x", "yh")]).astype(jnp.int32)

    whole = pl.BlockSpec((HALF, NZ * SLOTS * HD), lambda x: (0, 0))
    packed = pl.pallas_call(
        pack_kernel,
        grid=(NX,),
        out_shape=shape((NB, ROWS, HD), BF16),
        in_specs=[
            SMEM,
            SMEM,
            whole,
            whole,
            whole,
            pl.BlockSpec((2, BS), lambda x: (0, 0)),
            pl.BlockSpec((2, NBR), lambda x: (0, 0)),
        ],
        out_specs=pl.BlockSpec((NB // NX, ROWS, HD), lambda x: (x, 0, 0)),
        scratch_shapes=[pltpu.VMEM((META, BS), F32)],
        compiler_params=FULL,
        name="pack",
    )(info, chain_of_block, queries, keys, values, key_valid.reshape(2, BS), neighbours)
    packed, out_grad = lax.optimization_barrier((packed, out_grad))
    rows = lax.all_to_all(packed, CHIPS, split_axis=0, concat_axis=0, tiled=True)
    grads = pl.pallas_call(
        pack_grad_kernel,
        out_shape=(shape((2, 2 * BS, HD), BF16),) * NX,
        in_specs=[SMEM, VMEM],
        out_specs=(VMEM,) * NX,
        compiler_params=FULL,
        name="pack_grad",
    )(info, out_grad)

    def along_x(pieces, onward):
        moved = []
        for d, piece in enumerate(pieces, 1):
            pairs = [(i, i ^ d) for i in range(NX) if (i ^ d if onward else i) < SLOTS // NYH]
            moved.append(lax.ppermute(piece, "x", pairs))
        return moved

    moved = along_x(grads[1:], True)
    rows, moved = lax.optimization_barrier((rows, moved))
    grads = [grads[0]] + moved
    came = lax.ppermute(jnp.stack([piece[1] for piece in grads]), "yh", swap)
    grads = [came] + grads
    other = lax.ppermute(rows, "c", swap)
    theirs = lax.dynamic_index_in_dim(
        rows.reshape(SIDES, NYL, NZ, ROWS, HD)[:, :, :, Q_AT:],
        1 - lax.axis_index("yl"),
        axis=1,
        keepdims=False,
    )
    lower = lax.ppermute(theirs.reshape(SIDES * NZ, QUARTER, HD), "yl", swap)
    mine = rows.reshape(NB // NZ, NZ, ROWS, HD)[:, 0, 2 * HALF : 2 * HALF + 4]
    far = other.reshape(NB // NZ, NZ, ROWS, HD)[:, 0, 2 * HALF : 2 * HALF + 4]
    lists = jnp.stack([mine, far]).astype(jnp.int32).reshape(2 * NB, HD)
    block = mine[:, 2:, :NBR].astype(jnp.int32)
    away = (block // 2 % 2 != lax.axis_index("c")).astype(jnp.int32)
    there = block // 4
    slots = away * (NB // 2) + there * 2 + block % 2
    lines = away * NB + there * 4 + 2 + block % 2
    near = jnp.concatenate([slots, lines], axis=-1).reshape(NB // 2, 2 * NBR)
    att_keep, att_swap, back, far, lower = attend(info, near, lists, chain_bias, rows, other, lower, *grads)

    came = lax.ppermute(far, "c", swap)
    lower_came = lax.ppermute(lower, "yl", swap)
    att_swap, came = lax.optimization_barrier((att_swap, came))
    att_came = lax.ppermute(att_swap, "yh", swap)
    sems = pltpu.SemaphoreType.DMA((PARTS,))
    back = pl.pallas_call(
        merge_kernel,
        out_shape=shape((NB, BACK, HD), BF16),
        in_specs=[SMEM, ANY, ANY, ANY],
        out_specs=ANY,
        scratch_shapes=[
            pltpu.VMEM((NB, 2 * HALF, HD), BF16),
            pltpu.VMEM((NB, 2 * HALF, HD), BF16),
            sems,
            sems,
            sems,
            pltpu.SemaphoreType.DMA((SIDES,)),
        ],
        input_output_aliases={1: 0},
        compiler_params=PARAMS,
        name="merge",
    )(info, back, came, lower_came)
    back, att_keep, att_came = lax.optimization_barrier((back, att_keep, att_came))
    back = lax.all_to_all(back, CHIPS, split_axis=0, concat_axis=0, tiled=True)
    moved = along_x([jnp.stack([att_keep[d], att_came[d]]) for d in range(1, NX)], False)
    flat = shape((HALF, NZ * SLOTS * HD), BF16)
    dq, dk, dv, attended = pl.pallas_call(
        unpack_kernel,
        out_shape=(flat, flat, flat, shape((2 * BS, SLOTS * HD), BF16)),
        in_specs=[SMEM] + [ANY] * 6,
        out_specs=(VMEM, VMEM, VMEM, ANY),
        scratch_shapes=[
            pltpu.VMEM((NB, BACK, HD), BF16),
            pltpu.SemaphoreType.DMA((SLOTS // NYH,)),
            pltpu.SemaphoreType.DMA((SIDES,)),
        ],
        compiler_params=PARAMS,
        name="unpack",
    )(info, back, att_keep, att_came, *moved)
    return attended, dq, dk, dv


def solution(mesh):
    grid = Mesh(mesh.devices.reshape(NX, NYH, NYL, NC, NZ), ("x", "yh", "yl", "c", "z"))
    res = ("x", "yh", "yl", "c")
    both = P(res + ("z",), None)
    return jax.shard_map(
        body,
        mesh=grid,
        in_specs=(both, both, both, P(res, "z"), P("z"), P(res), P(res), P(res, None)),
        out_specs=(P(res, "z"), both, both, both),
        check_vma=False,
    )
```

```python
import functools
import math

import jax
import jax.numpy as jnp
from jax import lax
from jax.experimental import pallas as pl
from jax.experimental.pallas import tpu as pltpu
from jax.sharding import Mesh, PartitionSpec as P

HD = 128
BS = 128
NBR = 16
HALF = 64
QUARTER = 32
NX, NYH, NYL, NC, NZ = 4, 2, 2, 2, 4
SLOTS = 6
META = 16
SIDES = NX * NYH
Q_AT = 2 * HALF + META
ROWS = Q_AT + QUARTER
BACK = 2 * HALF + QUARTER
NB = 64
QB = 16
SCALE = 1.0 / math.sqrt(HD)
LOG2E = math.log2(math.e)
CHIPS = ("x", "yh", "yl", "z")
PARTS = 4
ANY = pl.BlockSpec(memory_space=pl.ANY)
VMEM = pl.BlockSpec(memory_space=pltpu.VMEM)
SMEM = pl.BlockSpec(memory_space=pltpu.SMEM)
PARAMS = pltpu.CompilerParams(vmem_limit_bytes=50 * 1024 * 1024)
FULL = pltpu.CompilerParams(vmem_limit_bytes=62 * 1024 * 1024)
F32 = jnp.float32
BF16 = jnp.bfloat16


def chip_index(x, yh, yl, z):
    return ((x * NYH + yh) * NYL + yl) * NZ + z


def pack_kernel(info_ref, chain_ref, q_ref, k_ref, v_ref, valid_ref, near_ref, rows_ref, lists):
    x = pl.program_id(0)
    low = info_ref[1]

    @pl.when(x == 0)
    def _():
        lane = lax.broadcasted_iota(jnp.int32, (1, BS), 1)
        lists[...] = jnp.zeros((META, BS), F32)
        lists[0:2] = valid_ref[...].astype(F32)
        lists[2:4, 0:NBR] = near_ref[...].astype(F32)
        for half in range(2):
            line = lists[2 + half : 3 + half]
            chain = jnp.full((1, BS), chain_ref[half], jnp.int32).astype(F32)
            lists[2 + half : 3 + half] = jnp.where(lane == NBR, chain, line)

    @pl.when(x < SLOTS // NYH)
    def _():
        for yh in range(NYH):
            for z in range(NZ):
                start = pl.multiple_of((z * SLOTS + x * NYH + yh) * HD, HD)
                first, second = chip_index(0, yh, 0, z), chip_index(0, yh, 1, z)
                for t, ref in enumerate((k_ref, v_ref)):
                    piece = ref[:, pl.ds(start, HD)]
                    for dest in (first, second):
                        rows_ref[dest, t * HALF : (t + 1) * HALF] = piece
                query = q_ref[:, pl.ds(start, HD)]
                upper, lower = query[:QUARTER], query[QUARTER:]
                rows_ref[first, Q_AT:] = jnp.where(low == 0, upper, lower)
                rows_ref[second, Q_AT:] = jnp.where(low == 0, lower, upper)

    @pl.when(x >= SLOTS // NYH)
    def _():
        rows_ref[...] = jnp.zeros((NB // NX, ROWS, HD), BF16)

    held = lists[...].astype(BF16)
    for dest in range(NB // NX):
        rows_ref[dest, 2 * HALF : Q_AT] = held


def pack_grad_kernel(info_ref, g_ref, *grad_refs):
    x, yh = info_ref[2], info_ref[3]
    for d, ref in enumerate(grad_refs):
        first = jnp.minimum(x ^ d, SLOTS // NYH - 1) * NYH
        for n, side in enumerate((yh, 1 - yh)):
            ref[n] = g_ref[:, pl.ds(pl.multiple_of((first + side) * HD, HD), HD)]


def dot(a, b):
    return jnp.dot(a, b, preferred_element_type=F32)


def attention_kernel(
    info_ref,
    near_ref,
    lists_ref,
    bias_ref,
    rows_hbm,
    other_hbm,
    lower_hbm,
    grad_came_hbm,
    grad_0_hbm,
    grad_1_hbm,
    grad_2_hbm,
    grad_3_hbm,
    att_keep_hbm,
    att_swap_hbm,
    back_hbm,
    far_hbm,
    lower_out_hbm,
    *refs,
):
    (
        rows_ref,
        other_ref,
        lower_ref,
        lower_out_ref,
        grad_ref,
        att_ref,
        kv,
        kt,
        vt,
        mask,
        scores,
        weights,
        dprob_even,
        dprob_odd,
        stats,
        dkv,
        back_ref,
        far_ref,
        rows_sem,
        other_sem,
        lower_sem,
        grad_sem,
        att_sem,
        back_sem,
        far_sem,
    ) = refs
    core = info_ref[0]
    low = info_ref[1]
    x, yh = info_ref[2], info_ref[3]
    slot_here = x * NYH + yh
    dprob = (dprob_even, dprob_odd)
    bias = bias_ref[jnp.minimum(slot_here, SLOTS - 1)] * LOG2E
    part = NB // PARTS

    def chunk(k):
        return pl.ds(k * part, part)

    def copies(source, target, sems, lines):
        return [
            pltpu.make_async_copy(
                source.at[chunk(k), pl.ds(0, lines)], target.at[chunk(k)], sems.at[k]
            )
            for k in range(PARTS)
        ]

    rows_in = copies(rows_hbm, rows_ref, rows_sem, ROWS)
    other_in = copies(other_hbm, other_ref, other_sem, Q_AT)
    grad_pieces = []
    for d, ref in enumerate((grad_0_hbm, grad_1_hbm, grad_2_hbm, grad_3_hbm)):
        grad_pieces.append((ref.at[0], grad_came_hbm.at[d]))
    grads_in = []
    att_out = []
    for d, pieces in enumerate(grad_pieces):
        for n, (piece, side, att_hbm) in enumerate(
            ((pieces[0], yh, att_keep_hbm), (pieces[1], 1 - yh, att_swap_hbm))
        ):
            pair = (x ^ d) * NYH + side
            at = d * 2 + n
            grads_in.append(pltpu.make_async_copy(piece, grad_ref.at[pair], grad_sem.at[at]))
            att_out.append(pltpu.make_async_copy(att_ref.at[pair], att_hbm.at[d], att_sem.at[at]))
    lower_in = pltpu.make_async_copy(lower_hbm, lower_ref, lower_sem.at[0])
    lower_out = pltpu.make_async_copy(lower_out_ref, lower_out_hbm, lower_sem.at[1])
    for copy in rows_in + other_in + [lower_in] + grads_in:
        copy.start()

    def grad_block(i):
        start = pl.multiple_of((i % 2) * BS, BS)
        return grad_ref[i // 2, pl.ds(start, BS)]

    def fill(quad, base, ref):
        row = lax.broadcasted_iota(jnp.int32, (BS, BS), 0)
        same = row == lax.broadcasted_iota(jnp.int32, (BS, BS), 1)
        lines = ref[quad * 4, 2 * HALF : Q_AT].astype(F32)
        for half in range(2):
            src = quad * 4 + half * 2
            slot = base + quad * 2 + half
            k_block = jnp.concatenate([ref[src, :HALF], ref[src + 1, :HALF]], axis=0)
            v_block = jnp.concatenate(
                [ref[src, HALF : 2 * HALF], ref[src + 1, HALF : 2 * HALF]], axis=0
            )
            kv[slot] = jnp.concatenate([k_block, v_block], axis=1)
            kt[slot] = k_block.T
            vt[slot] = v_block.T
            dkv[slot] = jnp.zeros((BS, 2 * HD), F32)
            spread = jnp.where(same, jnp.broadcast_to(lines[half : half + 1], (BS, BS)), 0.0)
            shown = dot(spread.astype(BF16), jnp.ones((BS, BS), BF16))
            mask[slot] = jnp.where(shown == 1.0, 0.0, -jnp.inf)

    for base, ref, waits in ((0, rows_ref, rows_in), (NB // 2, other_ref, other_in)):
        for k, copy in enumerate(waits):
            copy.wait()

            def fill_one(m, _, base=base, ref=ref, k=k):
                fill(k * (part // 4) + m, base, ref)
                return 0

            lax.fori_loop(0, part // 4, fill_one, 0, unroll=2)
    lower_in.wait()
    for copy in grads_in:
        copy.wait()

    def diagonal(a, b):
        zero = jnp.zeros((HD, HD), BF16)
        return jnp.concatenate(
            [jnp.concatenate([a, zero], axis=1), jnp.concatenate([zero, b], axis=1)], axis=0
        )

    def place(i):
        pair = i // 2
        half = i % 2
        quad = pair * 2 + low
        return pair, half, quad

    def query_block(i):
        pair, half, quad = place(i)
        src = quad * 4 + half * 2
        low_src = pair * 4 + half * 2
        pieces = []
        for h in range(2):
            pieces += [rows_ref[src + h, Q_AT:], lower_ref[low_src + h]]
        return jnp.concatenate(pieces, axis=0)

    def listed(i, j):
        _, half, quad = place(i)
        return near_ref[quad * 2 + half, j]

    def chain_at(i, j):
        _, half, quad = place(i)
        return lists_ref[near_ref[quad * 2 + half, NBR + j], NBR]

    class Scores:
        def __init__(self, i, parity):
            _, half, quad = place(i)
            self.i = i
            self.chain = lists_ref[quad * 4 + 2 + half, NBR]
            self.into = diagonal(query_block(i).T, grad_block(i).T)
            self.dprob = dprob[parity]
            self.peak = jnp.full((8, BS), -jnp.inf, F32)

        def step(self, j):
            slot = listed(self.i, j)
            shift = jnp.where(chain_at(self.i, j) != self.chain, bias, 0.0)
            both = dot(kv[slot], self.into)
            score = both[:, :BS] * (SCALE * LOG2E) + (mask[slot] + shift)
            scores[j] = score
            self.dprob[j] = both[:, BS:]
            self.peak = jnp.maximum(self.peak, jnp.max(score.reshape(BS // 8, 8, BS), axis=0))

        def end(self):
            stats[0:1] = jnp.max(self.peak, axis=0, keepdims=True)

    class Mix:
        def __init__(self, i):
            self.i = i
            self.peak = stats[0:1]
            self.total = jnp.zeros((8, BS), F32)
            self.mixed = jnp.zeros((HD, BS), F32)
            self.held = []

        def step(self, j):
            row = jnp.exp2(scores[j] - self.peak)
            weights[j] = row
            self.total = self.total + jnp.sum(row.reshape(BS // 8, 8, BS), axis=0)
            self.held.append((row.astype(BF16), vt[listed(self.i, j)]))
            if j % 2:
                (r0, v0), (r1, v1) = self.held
                self.held = []
                self.mixed = self.mixed + dot(
                    jnp.concatenate([v0, v1], axis=1), jnp.concatenate([r0, r1], axis=0)
                )

        def end(self):
            total = jnp.sum(self.total, axis=0, keepdims=True)
            attended = (self.mixed / total).astype(BF16)
            pair, half, _ = place(self.i)
            att_ref[pair, pl.ds(pl.multiple_of(half * BS, BS), BS)] = attended.T
            grad = grad_block(self.i).T.astype(F32)
            stats[1:2] = jnp.sum(grad * attended.astype(F32), axis=0, keepdims=True)
            stats[2:3] = 1.0 / total

    class Back:
        def __init__(self, i, parity):
            self.i = i
            self.dprob = dprob[parity]
            self.delta = stats[1:2]
            self.inverse = stats[2:3]
            self.out_of = diagonal(query_block(i), grad_block(i))
            self.dqt = jnp.zeros((HD, BS), F32)
            self.held = []

        def step(self, j):
            slot = listed(self.i, j)
            probs = weights[j] * self.inverse
            dscore = (probs * (self.dprob[j] - self.delta)).astype(BF16)
            both = jnp.concatenate([dscore, probs.astype(BF16)], axis=1)
            dkv[slot] += dot(both, self.out_of)
            self.held.append((dscore, kt[slot]))
            if j % 2:
                (s0, k0), (s1, k1) = self.held
                self.held = []
                self.dqt = self.dqt + dot(
                    jnp.concatenate([k0, k1], axis=1), jnp.concatenate([s0, s1], axis=0)
                )

        def end(self):
            pair, half, quad = place(self.i)
            dq = (self.dqt * SCALE).astype(BF16).T
            for h in range(2):
                at = h * HALF
                back_ref[quad * 4 + half * 2 + h, 2 * HALF :] = dq[at : at + QUARTER]
                lower_out_ref[pair * 4 + half * 2 + h] = dq[at + QUARTER : at + HALF]

    def together(*stages):
        for j in range(NBR):
            for stage in stages:
                stage.step(j)
        for stage in stages:
            stage.end()

    together(Scores(0, 0))
    together(Mix(0), Scores(1, 1))

    def rounds(r, _):
        for parity in range(2):
            i = r * 2 + parity
            together(Back(i, parity), Mix(i + 1), Scores(i + 2, parity))
        return 0

    lax.fori_loop(0, QB // 2 - 1, rounds, 0)
    together(Back(QB - 2, 0), Mix(QB - 1))
    together(Back(QB - 1, 1))

    for copy in att_out + [lower_out]:
        copy.start()
    far_out = copies(far_ref, far_hbm, far_sem, 2 * HALF)
    back_out = copies(back_ref, back_hbm, back_sem, BACK)

    def drain(b, base, target):
        for t, scale in enumerate((SCALE, 1.0)):
            block = (dkv[base + b, :, t * HD : (t + 1) * HD] * scale).astype(BF16)
            rows = slice(t * HALF, (t + 1) * HALF)
            for h in range(2):
                target[b * 2 + h, rows] = block[h * HALF : (h + 1) * HALF]

    for base, target, outs in ((NB // 2, far_ref, far_out), (0, back_ref, back_out)):
        for k, copy in enumerate(outs):

            def drain_one(m, _, base=base, target=target, k=k):
                drain(k * (part // 2) + m, base, target)
                return 0

            lax.fori_loop(0, part // 2, drain_one, 0)
            copy.start()
    for copy in att_out + [lower_out] + far_out + back_out:
        copy.wait()


def merge_kernel(
    info_ref,
    back_hbm,
    came_hbm,
    lower_hbm,
    out_hbm,
    back_ref,
    came_ref,
    back_sem,
    came_sem,
    out_sem,
    lower_sem,
):
    other = 1 - info_ref[1]
    each = NB // PARTS
    near = slice(0, 2 * HALF)
    copies = []
    for k in range(PARTS):
        part = pl.ds(k * each, each)
        copies.append(
            (
                pltpu.make_async_copy(
                    back_hbm.at[part, near], back_ref.at[part], back_sem.at[k]
                ),
                pltpu.make_async_copy(came_hbm.at[part], came_ref.at[part], came_sem.at[k]),
                pltpu.make_async_copy(back_ref.at[part], out_hbm.at[part, near], out_sem.at[k]),
            )
        )
    lower = []
    for n in range(SIDES):
        target = out_hbm.at[pl.ds((n * 2 + other) * NZ, NZ), slice(2 * HALF, BACK)]
        source = lower_hbm.at[pl.ds(n * NZ, NZ)]
        lower.append(pltpu.make_async_copy(source, target, lower_sem.at[n]))
    for mine, came, _ in copies:
        mine.start()
        came.start()
    for copy in lower:
        copy.start()
    for k, (mine, came, out) in enumerate(copies):
        mine.wait()
        came.wait()

        def add(m, _, k=k):
            n = k * each + m
            back_ref[n] = (back_ref[n].astype(F32) + came_ref[n].astype(F32)).astype(BF16)
            return 0

        lax.fori_loop(0, each, add, 0, unroll=4)
        out.start()
    for _, _, out in copies:
        out.wait()
    for copy in lower:
        copy.wait()


def join(info_ref, pieces, out_hbm, sems, act):
    x, yh = info_ref[2], info_ref[3]
    for d, pair in enumerate(pieces):
        first = (x ^ d) * NYH

        @pl.when(first < SLOTS)
        def _(d=d, pair=pair, first=first):
            for n, side in enumerate((yh, 1 - yh)):
                lane = pl.ds(pl.multiple_of((first + side) * HD, HD), HD)
                act(pltpu.make_async_copy(pair[n], out_hbm.at[:, lane], sems.at[d * 2 + n]))


def unpack_kernel(
    info_ref,
    rows_hbm,
    keep_hbm,
    came_hbm,
    one_hbm,
    two_hbm,
    three_hbm,
    dq_ref,
    dk_ref,
    dv_ref,
    att_hbm,
    rows_ref,
    sems,
    att_sems,
):
    pieces = [(keep_hbm.at[0], came_hbm.at[0])]
    for ref in (one_hbm, two_hbm, three_hbm):
        pieces.append((ref.at[0], ref.at[1]))
    join(info_ref, pieces, att_hbm, att_sems, lambda copy: copy.start())
    low = info_ref[1]
    each = NB // NX
    copies = [
        pltpu.make_async_copy(
            rows_hbm.at[pl.ds(x * each, each)], rows_ref.at[pl.ds(x * each, each)], sems.at[x]
        )
        for x in range(SLOTS // NYH)
    ]
    for copy in copies:
        copy.start()
    for x, copy in enumerate(copies):
        copy.wait()
        for yh in range(NYH):
            for z in range(NZ):
                head = z * SLOTS + x * NYH + yh
                lane = slice(head * HD, (head + 1) * HD)
                zero = chip_index(x, yh, 0, z)
                one = chip_index(x, yh, 1, z)
                dq_ref[:QUARTER, lane] = rows_ref[zero + low * NZ, 2 * HALF :]
                dq_ref[QUARTER:, lane] = rows_ref[zero + (1 - low) * NZ, 2 * HALF :]
                for t, ref in enumerate((dk_ref, dv_ref)):
                    part = slice(t * HALF, (t + 1) * HALF)
                    both = rows_ref[zero, part].astype(F32) + rows_ref[one, part].astype(F32)
                    ref[:, lane] = both.astype(BF16)
    join(info_ref, pieces, att_hbm, att_sems, lambda copy: copy.wait())


def shape(dims, dtype):
    return jax.ShapeDtypeStruct(dims, dtype)


def attend(*operands):
    four = shape((NX, 2 * BS, HD), BF16)
    table = pltpu.VMEM((NB, BS, HD), BF16)
    near = pltpu.VMEM((NBR, BS, BS), F32)
    sems = pltpu.SemaphoreType.DMA((PARTS,))
    return pl.pallas_call(
        attention_kernel,
        out_shape=(
            four,
            four,
            shape((NB, BACK, HD), BF16),
            shape((NB, 2 * HALF, HD), BF16),
            shape((SIDES * NZ, QUARTER, HD), BF16),
        ),
        in_specs=[SMEM] * 4 + [ANY] * 8,
        out_specs=(ANY,) * 5,
        scratch_shapes=[
            pltpu.VMEM((NB, ROWS, HD), BF16),
            pltpu.VMEM((NB, Q_AT, HD), BF16),
            pltpu.VMEM((SIDES * NZ, QUARTER, HD), BF16),
            pltpu.VMEM((SIDES * NZ, QUARTER, HD), BF16),
            pltpu.VMEM((SIDES, 2 * BS, HD), BF16),
            pltpu.VMEM((SIDES, 2 * BS, HD), BF16),
            pltpu.VMEM((NB, BS, 2 * HD), BF16),
            table,
            table,
            pltpu.VMEM((NB, BS, BS), F32),
            near,
            near,
            near,
            near,
            pltpu.VMEM((8, BS), F32),
            pltpu.VMEM((NB, BS, 2 * HD), F32),
            pltpu.VMEM((NB, BACK, HD), BF16),
            pltpu.VMEM((NB, 2 * HALF, HD), BF16),
            sems,
            sems,
            pltpu.SemaphoreType.DMA((2,)),
            pltpu.SemaphoreType.DMA((SIDES,)),
            pltpu.SemaphoreType.DMA((SIDES,)),
            sems,
            sems,
        ],
        compiler_params=PARAMS,
        name="attention",
    )(*operands)


def body(queries, keys, values, out_grad, chain_bias, chain_of_block, key_valid, neighbours):
    swap = [(0, 1), (1, 0)]
    info = jnp.stack([lax.axis_index(name) for name in ("c", "yl", "x", "yh")]).astype(jnp.int32)

    whole = pl.BlockSpec((HALF, NZ * SLOTS * HD), lambda x: (0, 0))
    packed = pl.pallas_call(
        pack_kernel,
        grid=(NX,),
        out_shape=shape((NB, ROWS, HD), BF16),
        in_specs=[
            SMEM,
            SMEM,
            whole,
            whole,
            whole,
            pl.BlockSpec((2, BS), lambda x: (0, 0)),
            pl.BlockSpec((2, NBR), lambda x: (0, 0)),
        ],
        out_specs=pl.BlockSpec((NB // NX, ROWS, HD), lambda x: (x, 0, 0)),
        scratch_shapes=[pltpu.VMEM((META, BS), F32)],
        compiler_params=FULL,
        name="pack",
    )(info, chain_of_block, queries, keys, values, key_valid.reshape(2, BS), neighbours)
    packed, out_grad = lax.optimization_barrier((packed, out_grad))
    rows = lax.all_to_all(packed, CHIPS, split_axis=0, concat_axis=0, tiled=True)
    grads = pl.pallas_call(
        pack_grad_kernel,
        out_shape=(shape((2, 2 * BS, HD), BF16),) * NX,
        in_specs=[SMEM, VMEM],
        out_specs=(VMEM,) * NX,
        compiler_params=FULL,
        name="pack_grad",
    )(info, out_grad)

    def along_x(pieces, onward):
        moved = []
        for d, piece in enumerate(pieces, 1):
            pairs = [(i, i ^ d) for i in range(NX) if (i ^ d if onward else i) < SLOTS // NYH]
            moved.append(lax.ppermute(piece, "x", pairs))
        return moved

    moved = along_x(grads[1:], True)
    rows, moved = lax.optimization_barrier((rows, moved))
    grads = [grads[0]] + moved
    came = lax.ppermute(jnp.stack([piece[1] for piece in grads]), "yh", swap)
    grads = [came] + grads
    other = lax.ppermute(rows, "c", swap)
    theirs = lax.dynamic_index_in_dim(
        rows.reshape(SIDES, NYL, NZ, ROWS, HD)[:, :, :, Q_AT:],
        1 - lax.axis_index("yl"),
        axis=1,
        keepdims=False,
    )
    lower = lax.ppermute(theirs.reshape(SIDES * NZ, QUARTER, HD), "yl", swap)
    mine = rows.reshape(NB // NZ, NZ, ROWS, HD)[:, 0, 2 * HALF : 2 * HALF + 4]
    far = other.reshape(NB // NZ, NZ, ROWS, HD)[:, 0, 2 * HALF : 2 * HALF + 4]
    lists = jnp.stack([mine, far]).astype(jnp.int32).reshape(2 * NB, HD)
    block = mine[:, 2:, :NBR].astype(jnp.int32)
    away = (block // 2 % 2 != lax.axis_index("c")).astype(jnp.int32)
    there = block // 4
    slots = away * (NB // 2) + there * 2 + block % 2
    lines = away * NB + there * 4 + 2 + block % 2
    near = jnp.concatenate([slots, lines], axis=-1).reshape(NB // 2, 2 * NBR)
    att_keep, att_swap, back, far, lower = attend(info, near, lists, chain_bias, rows, other, lower, *grads)

    came = lax.ppermute(far, "c", swap)
    lower_came = lax.ppermute(lower, "yl", swap)
    att_came = lax.ppermute(att_swap, "yh", swap)
    sems = pltpu.SemaphoreType.DMA((PARTS,))
    back = pl.pallas_call(
        merge_kernel,
        out_shape=shape((NB, BACK, HD), BF16),
        in_specs=[SMEM, ANY, ANY, ANY],
        out_specs=ANY,
        scratch_shapes=[
            pltpu.VMEM((NB, 2 * HALF, HD), BF16),
            pltpu.VMEM((NB, 2 * HALF, HD), BF16),
            sems,
            sems,
            sems,
            pltpu.SemaphoreType.DMA((SIDES,)),
        ],
        input_output_aliases={1: 0},
        compiler_params=PARAMS,
        name="merge",
    )(info, back, came, lower_came)
    back, att_keep, att_came = lax.optimization_barrier((back, att_keep, att_came))
    back = lax.all_to_all(back, CHIPS, split_axis=0, concat_axis=0, tiled=True)
    moved = along_x([jnp.stack([att_keep[d], att_came[d]]) for d in range(1, NX)], False)
    flat = shape((HALF, NZ * SLOTS * HD), BF16)
    dq, dk, dv, attended = pl.pallas_call(
        unpack_kernel,
        out_shape=(flat, flat, flat, shape((2 * BS, SLOTS * HD), BF16)),
        in_specs=[SMEM] + [ANY] * 6,
        out_specs=(VMEM, VMEM, VMEM, ANY),
        scratch_shapes=[
            pltpu.VMEM((NB, BACK, HD), BF16),
            pltpu.SemaphoreType.DMA((SLOTS // NYH,)),
            pltpu.SemaphoreType.DMA((SIDES,)),
        ],
        compiler_params=PARAMS,
        name="unpack",
    )(info, back, att_keep, att_came, *moved)
    return attended, dq, dk, dv


def solution(mesh):
    grid = Mesh(mesh.devices.reshape(NX, NYH, NYL, NC, NZ), ("x", "yh", "yl", "c", "z"))
    res = ("x", "yh", "yl", "c")
    both = P(res + ("z",), None)
    return jax.shard_map(
        body,
        mesh=grid,
        in_specs=(both, both, both, P(res, "z"), P("z"), P(res), P(res), P(res, None)),
        out_specs=(P(res, "z"), both, both, both),
        check_vma=False,
    )
```
